32 devices in a mesh: seq: 8 (over y, x, core), tensor: 4 (over z).
Axes of the slice: x: 2, y: 2, z: 4, core: 2. Of those that a mesh axis runs over, the one named last changes fastest.
Arguments:
- tokens: bfloat16 [4096, 4096], P('seq', 'tensor'), may hold values from -6 to 6
- norm_gain: float32 [4096], replicated, may hold values from 0.1 to 1.9
- w_query: bfloat16 [4096, 4096], P('seq', 'tensor'), may hold values from -0.09375 to 0.09375
- w_key: bfloat16 [4096, 4096], P('seq', 'tensor'), may hold values from -0.09375 to 0.09375
- w_value: bfloat16 [4096, 4096], P('seq', 'tensor'), may hold values from -0.09375 to 0.09375
- out_gain: float32 [4096], P('tensor'), may hold values from 0.1 to 1.9
- carried: float32 [32, 128, 128], P('tensor'), may hold values from -384 to 384
Outputs:
- attended: bfloat16 [4096, 4096], P('seq', 'tensor')
- final_state: float32 [32, 128, 128], P('tensor')
The draws below stay inside these ranges and needn't reach their ends.
All inputs are finite; a program needn't handle non-finite values.
Results may differ from the reference program's by a relative error of at most 0.009.
Values may be sent and summed in bfloat16 or wider, within the bound.
A program may use at most 64 MiB of HBM per device.

```python
import jax
import jax.numpy as jnp
from jax import lax

D = 4096
H = 32
HD = 128
BLOCK = 512
TOKENS = 4096


def block_scale(own_key, shape, shards, least, high):
    level = 1.0
    for axis_at, blocks in shards:
        steps = jax.random.uniform(jax.random.fold_in(jax.random.fold_in(own_key, 6), axis_at), (blocks,), jnp.float32, least / len(shards), high / len(shards))
        level = level * jnp.repeat(jnp.exp(steps), shape[axis_at] // blocks).reshape((-1,) + (1,) * (len(shape) - 1 - axis_at))
    return level


def bell_draw(rng, shape, deviation, reach, pieces=(), kind=jnp.bfloat16):
    result = deviation * jax.random.normal(rng, shape, jnp.float32)
    if pieces:
        result = result * block_scale(rng, shape, pieces, -0.22, 0.18)
    return jnp.clip(result, -reach, reach).astype(kind)


def setup_inputs(seed: int = 0) -> dict:
    key_list = jax.random.split(jax.random.key(seed), 8)
    return {
        "tokens": bell_draw(key_list[0], (TOKENS, D), 1.0, 6.0, ((0, 8), (1, 4))),
        "norm_gain": jnp.clip(1.0 + 0.18 * jax.random.normal(key_list[1], (D,), jnp.float32), 0.1, 1.9),
        "w_query": bell_draw(key_list[2], (D, H * HD), D ** -0.5, 0.09375, ((0, 8), (1, 4))),
        "w_key": bell_draw(key_list[3], (D, H * HD), D ** -0.5, 0.09375, ((0, 8), (1, 4))),
        "w_value": bell_draw(key_list[4], (D, H * HD), D ** -0.5, 0.09375, ((0, 8), (1, 4))),
        "out_gain": jnp.clip(1.0 + 0.18 * jax.random.normal(key_list[5], (H * HD,), jnp.float32), 0.1, 1.9),
        "carried": bell_draw(key_list[6], (H, HD, HD), 64.0, 384.0, ((0, 4),), jnp.float32),
    }


def reference(tokens, norm_gain, w_query, w_key, w_value, out_gain, carried):
    xf = tokens.astype(jnp.float32)
    normed = (xf * lax.rsqrt(lax.optimization_barrier(jnp.mean(xf * xf, axis=1, keepdims=True)) + 1e-05) * norm_gain).astype(jnp.bfloat16)
    query = jnp.dot(normed, w_query, preferred_element_type=jnp.float32).astype(jnp.bfloat16)
    key = jnp.dot(normed, w_key, preferred_element_type=jnp.float32).astype(jnp.bfloat16)
    value = jnp.dot(normed, w_value, preferred_element_type=jnp.float32).astype(jnp.bfloat16)
    count = TOKENS // BLOCK
    query = query.reshape(count, BLOCK, H, HD).transpose(2, 0, 1, 3)
    key = key.reshape(count, BLOCK, H, HD).transpose(2, 0, 1, 3)
    value = value.reshape(count, BLOCK, H, HD).transpose(2, 0, 1, 3)
    gains = out_gain.reshape(H, HD)
    causal = jnp.tril(jnp.ones((BLOCK, BLOCK), jnp.float32))

    def one_head(packed):
        qh, kh, vh, start, gain = packed

        def step(state, blocks):
            qb, kb, vb = blocks
            inter = jnp.dot(qb.astype(jnp.float32), state, precision=lax.Precision.HIGHEST)
            scores = (jnp.dot(qb, kb.T, preferred_element_type=jnp.float32) * causal).astype(jnp.bfloat16)
            raw = inter + jnp.dot(scores, vb, preferred_element_type=jnp.float32)
            out = raw * lax.rsqrt(lax.optimization_barrier(jnp.mean(raw * raw, axis=1, keepdims=True)) + 1e-06) * gain
            state = state + jnp.dot(kb.T, vb, preferred_element_type=jnp.float32)
            return (state, out.astype(jnp.bfloat16))
        state, outs = lax.scan(step, start, (qh, kh, vh))
        return (outs, state)
    outs, states = lax.map(one_head, (query, key, value, carried, gains))
    attended = outs.transpose(1, 2, 0, 3).reshape(TOKENS, H * HD)
    return (attended, states)
```

```python
import functools

import jax
import jax.numpy as jnp
from jax import lax
from jax.experimental import pallas as pl
from jax.experimental.pallas import tpu as pltpu
from jax.sharding import PartitionSpec as P

BLOCK = 512
MESH = pl.DeviceIdType.MESH
GROUP = 256
PARTS = 4
AHEAD = 3


def add_rows(normed, pieces):
    return tuple((jnp.dot(normed, piece, preferred_element_type=jnp.float32) for piece in pieces))


def shards(tokens, norm_gain, w_query, w_key, w_value, out_gain, carried):
    whole = lax.all_gather(tokens, "tensor", axis=1, tiled=True)
    xf = whole.astype(jnp.float32)
    normed = (xf * lax.rsqrt(jnp.mean(xf * xf, axis=1, keepdims=True) + 1e-05) * norm_gain).astype(
        jnp.bfloat16
    )
    rows = normed.shape[0]
    width = w_query.shape[1]
    size = carried.shape[1]
    heads = width // size
    qsum, ksum, vsum = add_rows(
        normed,
        (
            lax.all_gather(w_query, "seq", axis=0, tiled=True),
            lax.all_gather(w_key, "seq", axis=0, tiled=True),
            lax.all_gather(w_value, "seq", axis=0, tiled=True),
        ),
    )
    blocks = rows // BLOCK
    query = qsum.astype(jnp.bfloat16).reshape(blocks, BLOCK, heads, size)
    key = ksum.astype(jnp.bfloat16).reshape(blocks, BLOCK, heads, size)
    value = vsum.astype(jnp.bfloat16).reshape(blocks, BLOCK, heads, size)
    block_state = jnp.einsum("nthd,nthe->nhde", key, value, preferred_element_type=jnp.float32)
    local_total = jnp.sum(block_state, axis=0)
    zero_state = jnp.zeros_like(local_total)
    mine = lax.axis_index("seq")
    piece = lax.all_gather(
        local_total[None].astype(jnp.bfloat16), "seq", axis=0, tiled=True
    ).astype(jnp.float32)
    where = jnp.arange(piece.shape[0], dtype=jnp.int32)
    keep = (where < mine).astype(jnp.float32)
    before = zero_state + jnp.sum(keep[:, None, None, None] * piece, axis=0)
    total = zero_state + jnp.sum(piece, axis=0)
    start_state = carried + before
    running = jnp.cumsum(block_state, axis=0) - block_state
    priors = start_state[None] + running
    inter = jnp.einsum(
        "nthd,nhde->nthe", query.astype(jnp.float32), priors, precision=lax.Precision.HIGHEST
    )
    causal = jnp.tril(jnp.ones((BLOCK, BLOCK), jnp.float32))
    scores = jnp.einsum("nthd,nshd->nhts", query, key, preferred_element_type=jnp.float32)
    weights = (scores * causal).astype(jnp.bfloat16)
    intra = jnp.einsum("nhts,nshe->nthe", weights, value, preferred_element_type=jnp.float32)
    raw = inter + intra
    normal = (
        raw
        * lax.rsqrt(jnp.mean(raw * raw, axis=3, keepdims=True) + 1e-06)
        * out_gain.reshape(heads, size)
    )
    attended = normal.astype(jnp.bfloat16).reshape(rows, width)
    return (attended, carried + total)


def dot(a, b, dims=((1,), (0,))):
    return lax.dot_general(a, b, (dims, ((), ())), preferred_element_type=jnp.float32)


def kernel(
    depth_z,
    tokens,
    norm_gain,
    w_query,
    w_key,
    w_value,
    out_gain,
    carried,
    attended,
    final,
    tok,
    normed,
    buf,
    proj,
    state_out,
    state_sib,
    sum_out,
    sum_in,
    prior,
    local_sem,
    w_send,
    w_recv,
    t_send,
    t_recv,
    s_send,
    s_recv,
):
    rows, shard = tokens.shape
    depth = w_query.shape[0]
    groups = w_query.shape[1] // GROUP
    size = carried.shape[1]
    heads = carried.shape[0]
    per = GROUP // size
    half = heads // 2
    early = 2 * groups
    chunks = 3 * groups
    part = rows // PARTS
    hops = depth_z - 1

    seq = lax.axis_index("seq")
    z = lax.axis_index("tensor")
    c = seq % 2
    x = (seq // 2) % 2
    y = seq // 4
    sib = y * 4 + x * 2 + (1 - c)
    xn = y * 4 + (1 - x) * 2 + c
    yn = (1 - y) * 4 + x * 2 + c
    diag = (1 - y) * 4 + (1 - x) * 2 + c
    x_sib = y * 4 + (1 - x) * 2 + (1 - c)
    y_sib = (1 - y) * 4 + x * 2 + (1 - c)
    diag_sib = (1 - y) * 4 + (1 - x) * 2 + (1 - c)

    tok_copy = pltpu.make_async_copy(tokens, tok.at[z], local_sem.at[chunks])
    tok_copy.start()
    own_copies = []
    for ch in range(chunks):
        if ch < early:
            ref, g = (w_key, w_value)[ch % 2], ch // 2
        else:
            ref, g = w_query, ch - early
        copy = pltpu.make_async_copy(
            ref.at[:, pl.ds(g * GROUP, GROUP)],
            buf.at[ch, pl.ds(pl.multiple_of(seq * depth, depth), depth), :],
            local_sem.at[ch],
        )
        copy.start()
        own_copies.append(copy)

    barrier = pltpu.get_barrier_semaphore()
    for other in (sib, xn, yn):
        pl.semaphore_signal(barrier, inc=1, device_id=(other, z), device_id_type=MESH)

    @pl.when(z > 0)
    def _():
        pl.semaphore_signal(barrier, inc=1, device_id=(seq, z - 1), device_id_type=MESH)

    @pl.when(z < depth_z - 1)
    def _():
        pl.semaphore_signal(barrier, inc=1, device_id=(seq, z + 1), device_id_type=MESH)

    pl.semaphore_wait(barrier, 3 + jnp.minimum(z, 1) + jnp.minimum(depth_z - 1 - z, 1))

    def piece(ch, kind, owner, target, first=0, count=None):
        count = depth if count is None else count
        at = buf.at[ch, pl.ds(pl.multiple_of(owner * depth + first, count), count), :]
        return pltpu.make_async_remote_copy(
            src_ref=at,
            dst_ref=at,
            send_sem=w_send.at[ch, kind],
            recv_sem=w_recv.at[ch, kind],
            device_id=(target, z),
            device_id_type=MESH,
        )

    mid = depth // 2

    def outgoing(ch, kind):
        places = (
            (seq, xn),
            (seq, yn),
            (seq, sib),
            (xn, yn, 0, mid),
            (yn, xn, mid, mid),
            (xn, sib),
            (yn, sib),
            (diag, sib),
        )
        return piece(ch, kind, *places[kind])

    def incoming(ch, kind):
        places = (
            (xn, xn),
            (yn, yn),
            (sib, sib),
            (diag, yn, 0, mid),
            (diag, xn, mid, mid),
            (x_sib, sib),
            (y_sib, sib),
            (diag_sib, sib),
        )
        return piece(ch, kind, *places[kind])

    def send_own(ch):
        for kind in (0, 1, 2):
            outgoing(ch, kind).start()

    def pass_near(ch):
        incoming(ch, 0).wait_recv()
        outgoing(ch, 3).start()
        outgoing(ch, 5).start()
        incoming(ch, 1).wait_recv()
        outgoing(ch, 4).start()
        outgoing(ch, 6).start()

    def pass_far(ch):
        incoming(ch, 3).wait_recv()
        incoming(ch, 4).wait_recv()
        outgoing(ch, 7).start()

    def complete(ch):
        for kind in (2, 5, 6, 7):
            incoming(ch, kind).wait_recv()

    def token_copy(way, hop, p, owner):
        at = tok.at[owner, pl.ds(pl.multiple_of(p * part, part), part), :]
        target = z + 1 if way == 0 else z - 1
        return pltpu.make_async_remote_copy(
            src_ref=at,
            dst_ref=at,
            send_sem=t_send.at[way, hop, p],
            recv_sem=t_recv.at[way, hop, p],
            device_id=(seq, target),
            device_id_type=MESH,
        )

    def token_step(t):
        hop, p = t // PARTS, t % PARTS

        @pl.when(z - 1 - hop >= 0)
        def _():
            token_copy(0, hop, p, z - 1 - hop).wait_recv()

            @pl.when(z < depth_z - 1)
            def _():
                token_copy(0, hop + 1, p, z - 1 - hop).start()

        @pl.when(z + 1 + hop < depth_z)
        def _():
            token_copy(1, hop, p, z + 1 + hop).wait_recv()

            @pl.when(z > 0)
            def _():
                token_copy(1, hop + 1, p, z + 1 + hop).start()

    own_copies[0].wait()
    send_own(0)
    tok_copy.wait()

    @pl.loop(0, PARTS)
    def _(p):
        @pl.when(z < depth_z - 1)
        def _():
            token_copy(0, 0, p, z).start()

        @pl.when(z > 0)
        def _():
            token_copy(1, 0, p, z).start()

    for ch in range(1, chunks):
        own_copies[ch].wait()
    for ch in range(1, AHEAD):
        send_own(ch)

    def normalise():
        step = 32

        @pl.loop(0, rows // step)
        def _(r):
            at = pl.ds(pl.multiple_of(r * step, step), step)
            squares = jnp.zeros((step, 1), jnp.float32)
            for k in range(depth_z):
                v = tok[k, at, :].astype(jnp.float32)
                squares = squares + jnp.sum(v * v, axis=1, keepdims=True)
            scale = lax.rsqrt(squares / (depth_z * shard) + 1e-05)
            for k in range(depth_z):
                v = tok[k, at, :].astype(jnp.float32)
                gain = norm_gain[:, k * shard : (k + 1) * shard]
                normed[at, k * shard : (k + 1) * shard] = (v * scale * gain).astype(jnp.bfloat16)

    def project(ch):
        complete(ch)
        proj[ch] = dot(normed[...], buf[ch]).astype(jnp.bfloat16)

    def early_chunk(ch):
        project(ch)

        @pl.when(ch % 2 == 1)
        def _():
            both = dot(proj[ch - 1], proj[ch], ((0,), (0,)))
            for e in range(per):
                st = both[e * size : (e + 1) * size, e * size : (e + 1) * size]
                state_out[ch // 2 * per + e] = st.astype(jnp.bfloat16)

    mine = pl.ds(c * half, half)
    theirs = pl.ds((1 - c) * half, half)

    def state_copy(k, source, target_ref, target):
        return pltpu.make_async_remote_copy(
            src_ref=source,
            dst_ref=target_ref,
            send_sem=s_send.at[k],
            recv_sem=s_recv.at[k],
            device_id=(target, z),
            device_id_type=MESH,
        )

    to_sib = state_copy(0, state_out, state_sib, sib)
    to_x = state_copy(1, sum_out.at[0], sum_in.at[0, mine], xn)
    x_to_sib = state_copy(2, sum_in.at[0, mine], sum_in.at[0, mine], sib)
    to_y = state_copy(3, sum_out.at[1], sum_in.at[1, mine], yn)
    y_to_sib = state_copy(4, sum_in.at[1, mine], sum_in.at[1, mine], sib)
    x_from_sib = state_copy(2, sum_in.at[0, theirs], sum_in.at[0, theirs], sib)
    y_from_sib = state_copy(4, sum_in.at[1, theirs], sum_in.at[1, theirs], sib)

    def wide(v):
        return v.astype(jnp.float32)

    def state_one():
        to_sib.start()

    def state_two():
        to_sib.wait_recv()
        sum_out[0] = (wide(state_out[mine]) + wide(state_sib[mine])).astype(jnp.bfloat16)
        to_x.start()

    def state_three():
        to_x.wait_recv()
        x_to_sib.start()
        sum_out[1] = (wide(sum_out[0]) + wide(sum_in[0, mine])).astype(jnp.bfloat16)
        to_y.start()

    def state_four():
        to_y.wait_recv()
        y_to_sib.start()

    def state_five():
        x_from_sib.wait_recv()
        y_from_sib.wait_recv()
        on_c = c.astype(jnp.float32)
        on_x = x.astype(jnp.float32)
        on_y = y.astype(jnp.float32)
        for h in range(heads):
            near = wide(state_sib[h])
            chip = (wide(state_out[h]) + near).astype(jnp.bfloat16)
            beside = wide(sum_in[0, h])
            row = (wide(chip) + beside).astype(jnp.bfloat16)
            far = wide(sum_in[1, h])
            start = carried[h]
            before = near * on_c + beside * on_x + far * on_y
            prior[h] = (start + before).astype(jnp.bfloat16)
            final[h] = start + (wide(row) + far)

    top = rows // 2

    def attend(g):
        at = lax.broadcasted_iota(jnp.int32, (top, top), 0)
        of = lax.broadcasted_iota(jnp.int32, (top, top), 1)
        causal = of <= at

        def masked(s):
            return jnp.where(causal, s, 0.0).astype(jnp.bfloat16)

        for e in range(per):
            cols = slice(e * size, (e + 1) * size)
            h = g * per + e
            start = prior[h]
            q0, q1 = proj[early + g, :top, cols], proj[early + g, top:, cols]
            k0, k1 = proj[2 * g, :top, cols], proj[2 * g, top:, cols]
            v0, v1 = proj[2 * g + 1, :top, cols], proj[2 * g + 1, top:, cols]
            across = ((1,), (1,))
            raw0 = dot(q0, start) + dot(masked(dot(q0, k0, across)), v0)
            raw1 = (
                dot(q1, start)
                + dot(dot(q1, k0, across).astype(jnp.bfloat16), v0)
                + dot(masked(dot(q1, k1, across)), v1)
            )
            gain = out_gain[:, h * size : (h + 1) * size]
            for first, raw in ((0, raw0), (top, raw1)):
                scale = lax.rsqrt(jnp.mean(raw * raw, axis=1, keepdims=True) + 1e-06)
                attended[first : first + top, h * size : (h + 1) * size] = (
                    raw * scale * gain
                ).astype(jnp.bfloat16)

    steps = hops * PARTS

    @pl.loop(0, chunks)
    def _(i):
        @pl.when(i + AHEAD < chunks)
        def _():
            send_own(i + AHEAD)

        pass_near(i)

        @pl.when(i > 0)
        def _():
            pass_far(i - 1)

        @pl.when(i < early)
        def _():
            @pl.loop(i * steps // early, (i + 1) * steps // early)
            def _(t):
                token_step(t)

        @pl.when(i == early - 1)
        def _():
            normalise()

        @pl.when((i >= early) & (i < chunks - 1))
        def _():
            k = i - early
            span = groups - 1

            @pl.loop(k * early // span, (k + 1) * early // span)
            def _(ch):
                early_chunk(ch)

    state_one()
    project(early)
    state_two()
    project(early + 1)
    state_three()
    state_four()
    state_five()
    for g in range(groups):
        if g == groups - 1:
            pass_far(chunks - 1)
        if g >= 2:
            project(early + g)
        attend(g)

    @pl.loop(0, chunks)
    def _(ch):
        for kind in range(8):
            outgoing(ch, kind).wait_send()

    @pl.loop(0, steps)
    def _(t):
        hop, p = t // PARTS, t % PARTS

        @pl.when((z < depth_z - 1) & (z - hop >= 0))
        def _():
            token_copy(0, hop, p, z - hop).wait_send()

        @pl.when((z > 0) & (z + hop < depth_z))
        def _():
            token_copy(1, hop, p, z + hop).wait_send()

    for copy in (to_sib, to_x, x_to_sib, to_y, y_to_sib):
        copy.wait_send()


def fused(depth_z, tokens, norm_gain, w_query, w_key, w_value, out_gain, carried):
    rows, shard = tokens.shape
    depth, width = w_query.shape
    features = norm_gain.shape[0]
    heads, size = carried.shape[0], carried.shape[1]
    chunks = 3 * (width // GROUP)
    any_spec = pl.BlockSpec(memory_space=pl.ANY)
    vmem_spec = pl.BlockSpec(memory_space=pltpu.VMEM)
    dma = pltpu.SemaphoreType.DMA
    return pl.pallas_call(
        functools.partial(kernel, depth_z),
        out_shape=(
            jax.ShapeDtypeStruct((rows, width), jnp.bfloat16),
            jax.ShapeDtypeStruct(carried.shape, jnp.float32),
        ),
        in_specs=[any_spec, vmem_spec, any_spec, any_spec, any_spec, vmem_spec, vmem_spec],
        out_specs=(vmem_spec, vmem_spec),
        scratch_shapes=[
            pltpu.VMEM((depth_z, rows, shard), jnp.bfloat16),
            pltpu.VMEM((rows, features), jnp.bfloat16),
            pltpu.VMEM((chunks, features, GROUP), jnp.bfloat16),
            pltpu.VMEM((chunks, rows, GROUP), jnp.bfloat16),
            pltpu.VMEM((heads, size, size), jnp.bfloat16),
            pltpu.VMEM((heads, size, size), jnp.bfloat16),
            pltpu.VMEM((2, heads // 2, size, size), jnp.bfloat16),
            pltpu.VMEM((2, heads, size, size), jnp.bfloat16),
            pltpu.VMEM((heads, size, size), jnp.bfloat16),
            dma((chunks + 1,)),
            dma((chunks, 8)),
            dma((chunks, 8)),
            dma((2, depth_z, PARTS)),
            dma((2, depth_z, PARTS)),
            dma((5,)),
            dma((5,)),
        ],
        compiler_params=pltpu.CompilerParams(
            collective_id=0, has_side_effects=True, vmem_limit_bytes=56 * 1024 * 1024
        ),
        cost_estimate=pl.CostEstimate(
            flops=6 * rows * features * width, bytes_accessed=8 * depth * width, transcendentals=0
        ),
    )(tokens, norm_gain[None], w_query, w_key, w_value, out_gain[None], carried)


def solution(mesh):
    square = mesh.shape["seq"] == 8

    def local(tokens, *rest):
        if square and tokens.shape[0] == BLOCK:
            return fused(mesh.shape["tensor"], tokens, *rest)
        return shards(tokens, *rest)

    return jax.shard_map(
        local,
        mesh=mesh,
        in_specs=(
            P("seq", "tensor"),
            P(),
            P("seq", "tensor"),
            P("seq", "tensor"),
            P("seq", "tensor"),
            P("tensor"),
            P("tensor", None, None),
        ),
        out_specs=(P("seq", "tensor"), P("tensor", None, None)),
        check_vma=False,
    )
```

```python
import functools

import jax
import jax.numpy as jnp
from jax import lax
from jax.experimental import pallas as pl
from jax.experimental.pallas import tpu as pltpu
from jax.sharding import PartitionSpec as P

BLOCK = 512
MESH = pl.DeviceIdType.MESH
GROUP = 256
PARTS = 4
AHEAD = 3
LAG = 2
LANES = 128


def add_rows(normed, pieces):
    return tuple((jnp.dot(normed, piece, preferred_element_type=jnp.float32) for piece in pieces))


def shards(tokens, norm_gain, w_query, w_key, w_value, out_gain, carried):
    whole = lax.all_gather(tokens, "tensor", axis=1, tiled=True)
    xf = whole.astype(jnp.float32)
    normed = (xf * lax.rsqrt(jnp.mean(xf * xf, axis=1, keepdims=True) + 1e-05) * norm_gain).astype(
        jnp.bfloat16
    )
    rows = normed.shape[0]
    width = w_query.shape[1]
    size = carried.shape[1]
    heads = width // size
    qsum, ksum, vsum = add_rows(
        normed,
        (
            lax.all_gather(w_query, "seq", axis=0, tiled=True),
            lax.all_gather(w_key, "seq", axis=0, tiled=True),
            lax.all_gather(w_value, "seq", axis=0, tiled=True),
        ),
    )
    blocks = rows // BLOCK
    query = qsum.astype(jnp.bfloat16).reshape(blocks, BLOCK, heads, size)
    key = ksum.astype(jnp.bfloat16).reshape(blocks, BLOCK, heads, size)
    value = vsum.astype(jnp.bfloat16).reshape(blocks, BLOCK, heads, size)
    block_state = jnp.einsum("nthd,nthe->nhde", key, value, preferred_element_type=jnp.float32)
    local_total = jnp.sum(block_state, axis=0)
    zero_state = jnp.zeros_like(local_total)
    mine = lax.axis_index("seq")
    piece = lax.all_gather(
        local_total[None].astype(jnp.bfloat16), "seq", axis=0, tiled=True
    ).astype(jnp.float32)
    where = jnp.arange(piece.shape[0], dtype=jnp.int32)
    keep = (where < mine).astype(jnp.float32)
    before = zero_state + jnp.sum(keep[:, None, None, None] * piece, axis=0)
    total = zero_state + jnp.sum(piece, axis=0)
    start_state = carried + before
    running = jnp.cumsum(block_state, axis=0) - block_state
    priors = start_state[None] + running
    inter = jnp.einsum(
        "nthd,nhde->nthe", query.astype(jnp.float32), priors, precision=lax.Precision.HIGHEST
    )
    causal = jnp.tril(jnp.ones((BLOCK, BLOCK), jnp.float32))
    scores = jnp.einsum("nthd,nshd->nhts", query, key, preferred_element_type=jnp.float32)
    weights = (scores * causal).astype(jnp.bfloat16)
    intra = jnp.einsum("nhts,nshe->nthe", weights, value, preferred_element_type=jnp.float32)
    raw = inter + intra
    normal = (
        raw
        * lax.rsqrt(jnp.mean(raw * raw, axis=3, keepdims=True) + 1e-06)
        * out_gain.reshape(heads, size)
    )
    attended = normal.astype(jnp.bfloat16).reshape(rows, width)
    return (attended, carried + total)


def dot(a, b, dims=((1,), (0,))):
    return lax.dot_general(a, b, (dims, ((), ())), preferred_element_type=jnp.float32)


def kernel(
    depth_z,
    tokens,
    norm_gain,
    w_query,
    w_key,
    w_value,
    out_gain,
    carried,
    attended,
    final,
    tok,
    scaled,
    squares,
    row_scale,
    buf,
    acc,
    proj,
    state_out,
    state_sib,
    sum_out,
    sum_in,
    prior,
    local_sem,
    w_send,
    w_recv,
    t_send,
    t_recv,
    s_send,
    s_recv,
):
    rows, shard = tokens.shape
    depth = w_query.shape[0]
    groups = w_query.shape[1] // GROUP
    size = carried.shape[1]
    heads = carried.shape[0]
    per = GROUP // size
    half = heads // 2
    early = 2 * groups
    chunks = 3 * groups
    part = rows // PARTS
    hops = depth_z - 1

    seq = lax.axis_index("seq")
    z = lax.axis_index("tensor")
    c = seq % 2
    x = (seq // 2) % 2
    y = seq // 4
    sib = y * 4 + x * 2 + (1 - c)
    xn = y * 4 + (1 - x) * 2 + c
    yn = (1 - y) * 4 + x * 2 + c
    diag = (1 - y) * 4 + (1 - x) * 2 + c
    x_sib = y * 4 + (1 - x) * 2 + (1 - c)
    y_sib = (1 - y) * 4 + x * 2 + (1 - c)
    diag_sib = (1 - y) * 4 + (1 - x) * 2 + (1 - c)

    tok_copy = pltpu.make_async_copy(tokens, tok.at[z], local_sem.at[chunks])
    tok_copy.start()
    own_copies = []
    for ch in range(chunks):
        if ch < early:
            ref, g = (w_key, w_value)[ch % 2], ch // 2
        else:
            ref, g = w_query, ch - early
        copy = pltpu.make_async_copy(
            ref.at[:, pl.ds(g * GROUP, GROUP)],
            buf.at[ch, pl.ds(pl.multiple_of(seq * depth, depth), depth), :],
            local_sem.at[ch],
        )
        copy.start()
        own_copies.append(copy)

    barrier = pltpu.get_barrier_semaphore()
    for other in (sib, xn, yn):
        pl.semaphore_signal(barrier, inc=1, device_id=(other, z), device_id_type=MESH)

    @pl.when(z > 0)
    def _():
        pl.semaphore_signal(barrier, inc=1, device_id=(seq, z - 1), device_id_type=MESH)

    @pl.when(z < depth_z - 1)
    def _():
        pl.semaphore_signal(barrier, inc=1, device_id=(seq, z + 1), device_id_type=MESH)

    pl.semaphore_wait(barrier, 3 + jnp.minimum(z, 1) + jnp.minimum(depth_z - 1 - z, 1))

    def piece(ch, kind, owner, target, first=0, count=None):
        count = depth if count is None else count
        at = buf.at[ch, pl.ds(pl.multiple_of(owner * depth + first, count), count), :]
        return pltpu.make_async_remote_copy(
            src_ref=at,
            dst_ref=at,
            send_sem=w_send.at[ch, kind],
            recv_sem=w_recv.at[ch, kind],
            device_id=(target, z),
            device_id_type=MESH,
        )

    mid = depth // 2

    def outgoing(ch, kind):
        places = (
            (seq, xn),
            (seq, yn),
            (seq, sib),
            (xn, yn, 0, mid),
            (yn, xn, mid, mid),
            (xn, sib),
            (yn, sib),
            (diag, sib),
        )
        return piece(ch, kind, *places[kind])

    def incoming(ch, kind):
        places = (
            (xn, xn),
            (yn, yn),
            (sib, sib),
            (diag, yn, 0, mid),
            (diag, xn, mid, mid),
            (x_sib, sib),
            (y_sib, sib),
            (diag_sib, sib),
        )
        return piece(ch, kind, *places[kind])

    def send_own(ch):
        for kind in (0, 1, 2):
            outgoing(ch, kind).start()

    def pass_near(ch):
        incoming(ch, 0).wait_recv()
        outgoing(ch, 3).start()
        outgoing(ch, 5).start()
        incoming(ch, 1).wait_recv()
        outgoing(ch, 4).start()
        outgoing(ch, 6).start()

    def pass_far(ch):
        incoming(ch, 3).wait_recv()
        incoming(ch, 4).wait_recv()
        outgoing(ch, 7).start()

    def complete(ch):
        for kind in (2, 5, 6, 7):
            incoming(ch, kind).wait_recv()

    def token_copy(way, hop, p, owner):
        at = tok.at[owner, pl.ds(pl.multiple_of(p * part, part), part), :]
        target = z + 1 if way == 0 else z - 1
        return pltpu.make_async_remote_copy(
            src_ref=at,
            dst_ref=at,
            send_sem=t_send.at[way, hop, p],
            recv_sem=t_recv.at[way, hop, p],
            device_id=(seq, target),
            device_id_type=MESH,
        )

    def token_step(t):
        hop, p = t // PARTS, t % PARTS

        @pl.when(z - 1 - hop >= 0)
        def _():
            token_copy(0, hop, p, z - 1 - hop).wait_recv()

            @pl.when(z < depth_z - 1)
            def _():
                token_copy(0, hop + 1, p, z - 1 - hop).start()

        @pl.when(z + 1 + hop < depth_z)
        def _():
            token_copy(1, hop, p, z + 1 + hop).wait_recv()

            @pl.when(z > 0)
            def _():
                token_copy(1, hop + 1, p, z + 1 + hop).start()

    own_copies[0].wait()
    send_own(0)
    tok_copy.wait()

    @pl.loop(0, PARTS)
    def _(p):
        @pl.when(z < depth_z - 1)
        def _():
            token_copy(0, 0, p, z).start()

        @pl.when(z > 0)
        def _():
            token_copy(1, 0, p, z).start()

    for ch in range(1, chunks):
        own_copies[ch].wait()
    for ch in range(1, AHEAD):
        send_own(ch)

    def convert(k):
        step = 32

        @pl.loop(0, rows // step)
        def _(r):
            at = pl.ds(pl.multiple_of(r * step, step), step)
            v = tok[k, at, :].astype(jnp.float32)
            scaled[k, at, :] = (v * norm_gain[k]).astype(jnp.bfloat16)
            v = v * v
            total = squares[at, :]
            for f in range(shard // LANES):
                total = total + v[:, f * LANES : (f + 1) * LANES]
            squares[at, :] = total

    def find_scale():
        mean = jnp.sum(squares[...], axis=1, keepdims=True) / (depth_z * shard)
        row_scale[...] = jnp.broadcast_to(lax.rsqrt(mean + 1e-05), (rows, GROUP))

    def accumulate(ch, k):
        at = pl.ds(pl.multiple_of(k * shard, shard), shard)
        acc[ch] += dot(scaled[k], buf[ch, at, :])

    def finish(ch):
        proj[ch] = (acc[ch] * row_scale[...]).astype(jnp.bfloat16)

        @pl.when((ch % 2 == 1) & (ch < early))
        def _():
            both = dot(proj[ch - 1], proj[ch], ((0,), (0,)))
            for e in range(per):
                st = both[e * size : (e + 1) * size, e * size : (e + 1) * size]
                state_out[ch // 2 * per + e] = st.astype(jnp.bfloat16)

    def begin(ch, first, last):
        complete(ch)
        acc[ch] = jnp.zeros((rows, GROUP), jnp.float32)

        @pl.loop(first, last)
        def _(k):
            accumulate(ch, k)

    def project(ch):
        begin(ch, 0, depth_z)
        finish(ch)

    mine = pl.ds(c * half, half)
    theirs = pl.ds((1 - c) * half, half)

    def state_copy(k, source, target_ref, target):
        return pltpu.make_async_remote_copy(
            src_ref=source,
            dst_ref=target_ref,
            send_sem=s_send.at[k],
            recv_sem=s_recv.at[k],
            device_id=(target, z),
            device_id_type=MESH,
        )

    to_sib = state_copy(0, state_out, state_sib, sib)
    to_x = state_copy(1, sum_out.at[0], sum_in.at[0, mine], xn)
    x_to_sib = state_copy(2, sum_in.at[0, mine], sum_in.at[0, mine], sib)
    to_y = state_copy(3, sum_out.at[1], sum_in.at[1, mine], yn)
    y_to_sib = state_copy(4, sum_in.at[1, mine], sum_in.at[1, mine], sib)
    x_from_sib = state_copy(2, sum_in.at[0, theirs], sum_in.at[0, theirs], sib)
    y_from_sib = state_copy(4, sum_in.at[1, theirs], sum_in.at[1, theirs], sib)

    def wide(v):
        return v.astype(jnp.float32)

    def state_one():
        to_sib.start()

    def state_two():
        to_sib.wait_recv()
        sum_out[0] = (wide(state_out[mine]) + wide(state_sib[mine])).astype(jnp.bfloat16)
        to_x.start()

    def state_three():
        to_x.wait_recv()
        x_to_sib.start()
        sum_out[1] = (wide(sum_out[0]) + wide(sum_in[0, mine])).astype(jnp.bfloat16)
        to_y.start()

    def state_four():
        to_y.wait_recv()
        y_to_sib.start()

    def state_five():
        x_from_sib.wait_recv()
        y_from_sib.wait_recv()
        on_c = c.astype(jnp.float32)
        on_x = x.astype(jnp.float32)
        on_y = y.astype(jnp.float32)
        for h in range(heads):
            near = wide(state_sib[h])
            chip = (wide(state_out[h]) + near).astype(jnp.bfloat16)
            beside = wide(sum_in[0, h])
            row = (wide(chip) + beside).astype(jnp.bfloat16)
            far = wide(sum_in[1, h])
            start = carried[h]
            before = near * on_c + beside * on_x + far * on_y
            prior[h] = (start + before).astype(jnp.bfloat16)
            final[h] = start + (wide(row) + far)

    top = rows // 2

    def attend(g):
        at = lax.broadcasted_iota(jnp.int32, (top, top), 0)
        of = lax.broadcasted_iota(jnp.int32, (top, top), 1)
        causal = of <= at

        def masked(s):
            return jnp.where(causal, s, 0.0).astype(jnp.bfloat16)

        for e in range(per):
            cols = slice(e * size, (e + 1) * size)
            h = g * per + e
            start = prior[h]
            q0, q1 = proj[early + g, :top, cols], proj[early + g, top:, cols]
            k0, k1 = proj[2 * g, :top, cols], proj[2 * g, top:, cols]
            v0, v1 = proj[2 * g + 1, :top, cols], proj[2 * g + 1, top:, cols]
            across = ((1,), (1,))
            raw0 = dot(q0, start) + dot(masked(dot(q0, k0, across)), v0)
            raw1 = (
                dot(q1, start)
                + dot(dot(q1, k0, across).astype(jnp.bfloat16), v0)
                + dot(masked(dot(q1, k1, across)), v1)
            )
            gain = out_gain[:, h * size : (h + 1) * size]
            for first, raw in ((0, raw0), (top, raw1)):
                scale = lax.rsqrt(jnp.mean(raw * raw, axis=1, keepdims=True) + 1e-06)
                attended[first : first + top, h * size : (h + 1) * size] = (
                    raw * scale * gain
                ).astype(jnp.bfloat16)

    steps = hops * PARTS

    squares[...] = jnp.zeros_like(squares)
    convert(z)

    @pl.loop(0, chunks)
    def _(i):
        @pl.when(i + AHEAD < chunks)
        def _():
            send_own(i + AHEAD)

        pass_near(i)

        @pl.when(i >= LAG)
        def _():
            pass_far(i - LAG)

        first = jnp.minimum(i * steps // early, steps)
        last = jnp.minimum((i + 1) * steps // early, steps)

        @pl.loop(first, last)
        def _(t):
            token_step(t)

        level = last // PARTS
        now = i - LAG - 1

        @pl.when(level > first // PARTS)
        def _():
            for k in (z - level, z + level):

                @pl.when((k >= 0) & (k < depth_z))
                def _(k=k):
                    convert(k)

                    @pl.loop(0, now)
                    def _(ch):
                        accumulate(ch, k)

            @pl.when(level == hops)
            def _():
                find_scale()

                @pl.loop(0, now)
                def _(ch):
                    finish(ch)

        @pl.when(now >= 0)
        def _():
            begin(now, jnp.maximum(z - level, 0), jnp.minimum(z + level + 1, depth_z))

            @pl.when(level == hops)
            def _():
                finish(now)

        @pl.when(i == early + LAG)
        def _():
            state_one()

    state_two()
    pass_far(chunks - 2)
    state_three()
    project(early + 1)
    state_four()
    pass_far(chunks - 1)
    state_five()
    for g in range(groups):
        if g >= 2:
            project(early + g)
        attend(g)

    @pl.loop(0, chunks)
    def _(ch):
        for kind in range(8):
            outgoing(ch, kind).wait_send()

    @pl.loop(0, steps)
    def _(t):
        hop, p = t // PARTS, t % PARTS

        @pl.when((z < depth_z - 1) & (z - hop >= 0))
        def _():
            token_copy(0, hop, p, z - hop).wait_send()

        @pl.when((z > 0) & (z + hop < depth_z))
        def _():
            token_copy(1, hop, p, z + hop).wait_send()

    for copy in (to_sib, to_x, x_to_sib, to_y, y_to_sib):
        copy.wait_send()


def fused(depth_z, tokens, norm_gain, w_query, w_key, w_value, out_gain, carried):
    rows, shard = tokens.shape
    depth, width = w_query.shape
    features = norm_gain.shape[0]
    heads, size = carried.shape[0], carried.shape[1]
    chunks = 3 * (width // GROUP)
    any_spec = pl.BlockSpec(memory_space=pl.ANY)
    vmem_spec = pl.BlockSpec(memory_space=pltpu.VMEM)
    dma = pltpu.SemaphoreType.DMA
    return pl.pallas_call(
        functools.partial(kernel, depth_z),
        out_shape=(
            jax.ShapeDtypeStruct((rows, width), jnp.bfloat16),
            jax.ShapeDtypeStruct(carried.shape, jnp.float32),
        ),
        in_specs=[any_spec, vmem_spec, any_spec, any_spec, any_spec, vmem_spec, vmem_spec],
        out_specs=(vmem_spec, vmem_spec),
        scratch_shapes=[
            pltpu.VMEM((depth_z, rows, shard), jnp.bfloat16),
            pltpu.VMEM((depth_z, rows, shard), jnp.bfloat16),
            pltpu.VMEM((rows, LANES), jnp.float32),
            pltpu.VMEM((rows, GROUP), jnp.float32),
            pltpu.VMEM((chunks, features, GROUP), jnp.bfloat16),
            pltpu.VMEM((chunks, rows, GROUP), jnp.float32),
            pltpu.VMEM((chunks, rows, GROUP), jnp.bfloat16),
            pltpu.VMEM((heads, size, size), jnp.bfloat16),
            pltpu.VMEM((heads, size, size), jnp.bfloat16),
            pltpu.VMEM((2, heads // 2, size, size), jnp.bfloat16),
            pltpu.VMEM((2, heads, size, size), jnp.bfloat16),
            pltpu.VMEM((heads, size, size), jnp.bfloat16),
            dma((chunks + 1,)),
            dma((chunks, 8)),
            dma((chunks, 8)),
            dma((2, depth_z, PARTS)),
            dma((2, depth_z, PARTS)),
            dma((5,)),
            dma((5,)),
        ],
        compiler_params=pltpu.CompilerParams(
            collective_id=0, has_side_effects=True, vmem_limit_bytes=56 * 1024 * 1024
        ),
        cost_estimate=pl.CostEstimate(
            flops=6 * rows * features * width, bytes_accessed=8 * depth * width, transcendentals=0
        ),
    )(tokens, norm_gain.reshape(depth_z, 1, shard), w_query, w_key, w_value, out_gain[None], carried)


def solution(mesh):
    square = mesh.shape["seq"] == 8

    def local(tokens, *rest):
        if square and tokens.shape[0] == BLOCK:
            return fused(mesh.shape["tensor"], tokens, *rest)
        return shards(tokens, *rest)

    return jax.shard_map(
        local,
        mesh=mesh,
        in_specs=(
            P("seq", "tensor"),
            P(),
            P("seq", "tensor"),
            P("seq", "tensor"),
            P("seq", "tensor"),
            P("tensor"),
            P("tensor", None, None),
        ),
        out_specs=(P("seq", "tensor"), P("tensor", None, None)),
        check_vma=False,
    )
```

```python
import functools

import jax
import jax.numpy as jnp
from jax import lax
from jax.experimental import pallas as pl
from jax.experimental.pallas import tpu as pltpu
from jax.sharding import PartitionSpec as P

BLOCK = 512
MESH = pl.DeviceIdType.MESH
GROUP = 256
PARTS = 4
AHEAD = 2
LAG = 2
LANES = 128


def add_rows(normed, pieces):
    return tuple((jnp.dot(normed, piece, preferred_element_type=jnp.float32) for piece in pieces))


def shards(tokens, norm_gain, w_query, w_key, w_value, out_gain, carried):
    whole = lax.all_gather(tokens, "tensor", axis=1, tiled=True)
    xf = whole.astype(jnp.float32)
    normed = (xf * lax.rsqrt(jnp.mean(xf * xf, axis=1, keepdims=True) + 1e-05) * norm_gain).astype(
        jnp.bfloat16
    )
    rows = normed.shape[0]
    width = w_query.shape[1]
    size = carried.shape[1]
    heads = width // size
    qsum, ksum, vsum = add_rows(
        normed,
        (
            lax.all_gather(w_query, "seq", axis=0, tiled=True),
            lax.all_gather(w_key, "seq", axis=0, tiled=True),
            lax.all_gather(w_value, "seq", axis=0, tiled=True),
        ),
    )
    blocks = rows // BLOCK
    query = qsum.astype(jnp.bfloat16).reshape(blocks, BLOCK, heads, size)
    key = ksum.astype(jnp.bfloat16).reshape(blocks, BLOCK, heads, size)
    value = vsum.astype(jnp.bfloat16).reshape(blocks, BLOCK, heads, size)
    block_state = jnp.einsum("nthd,nthe->nhde", key, value, preferred_element_type=jnp.float32)
    local_total = jnp.sum(block_state, axis=0)
    zero_state = jnp.zeros_like(local_total)
    mine = lax.axis_index("seq")
    piece = lax.all_gather(
        local_total[None].astype(jnp.bfloat16), "seq", axis=0, tiled=True
    ).astype(jnp.float32)
    where = jnp.arange(piece.shape[0], dtype=jnp.int32)
    keep = (where < mine).astype(jnp.float32)
    before = zero_state + jnp.sum(keep[:, None, None, None] * piece, axis=0)
    total = zero_state + jnp.sum(piece, axis=0)
    start_state = carried + before
    running = jnp.cumsum(block_state, axis=0) - block_state
    priors = start_state[None] + running
    inter = jnp.einsum(
        "nthd,nhde->nthe", query.astype(jnp.float32), priors, precision=lax.Precision.HIGHEST
    )
    causal = jnp.tril(jnp.ones((BLOCK, BLOCK), jnp.float32))
    scores = jnp.einsum("nthd,nshd->nhts", query, key, preferred_element_type=jnp.float32)
    weights = (scores * causal).astype(jnp.bfloat16)
    intra = jnp.einsum("nhts,nshe->nthe", weights, value, preferred_element_type=jnp.float32)
    raw = inter + intra
    normal = (
        raw
        * lax.rsqrt(jnp.mean(raw * raw, axis=3, keepdims=True) + 1e-06)
        * out_gain.reshape(heads, size)
    )
    attended = normal.astype(jnp.bfloat16).reshape(rows, width)
    return (attended, carried + total)


def dot(a, b, dims=((1,), (0,))):
    return lax.dot_general(a, b, (dims, ((), ())), preferred_element_type=jnp.float32)


def kernel(
    depth_z,
    tokens,
    norm_gain,
    w_query,
    w_key,
    w_value,
    out_gain,
    carried,
    attended_out,
    final_out,
    tok,
    scaled,
    squares,
    row_scale,
    buf,
    acc,
    proj,
    state_out,
    state_sib,
    sum_out,
    sum_in,
    prior,
    local_sem,
    w_send,
    w_recv,
    t_send,
    t_recv,
    s_send,
    s_recv,
    attended,
    final,
    o_sem,
):
    rows, shard = tokens.shape
    depth = w_query.shape[0]
    groups = w_query.shape[1] // GROUP
    size = carried.shape[1]
    heads = carried.shape[0]
    per = GROUP // size
    half = heads // 2
    early = 2 * groups
    chunks = 3 * groups
    part = rows // PARTS
    hops = depth_z - 1

    seq = lax.axis_index("seq")
    z = lax.axis_index("tensor")
    c = seq % 2
    x = (seq // 2) % 2
    y = seq // 4
    sib = y * 4 + x * 2 + (1 - c)
    xn = y * 4 + (1 - x) * 2 + c
    yn = (1 - y) * 4 + x * 2 + c
    diag = (1 - y) * 4 + (1 - x) * 2 + c
    x_sib = y * 4 + (1 - x) * 2 + (1 - c)
    y_sib = (1 - y) * 4 + x * 2 + (1 - c)
    diag_sib = (1 - y) * 4 + (1 - x) * 2 + (1 - c)

    tok_copy = pltpu.make_async_copy(tokens, tok.at[z], local_sem.at[chunks])
    tok_copy.start()
    own_copies = []
    for ch in range(chunks):
        if ch < early:
            ref, g = (w_key, w_value)[ch % 2], ch // 2
        else:
            ref, g = w_query, ch - early
        copy = pltpu.make_async_copy(
            ref.at[:, pl.ds(g * GROUP, GROUP)],
            buf.at[ch, pl.ds(pl.multiple_of(seq * depth, depth), depth), :],
            local_sem.at[ch],
        )
        copy.start()
        own_copies.append(copy)

    barrier = pltpu.get_barrier_semaphore()
    for other in (sib, xn, yn):
        pl.semaphore_signal(barrier, inc=1, device_id=(other, z), device_id_type=MESH)

    @pl.when(z > 0)
    def _():
        pl.semaphore_signal(barrier, inc=1, device_id=(seq, z - 1), device_id_type=MESH)

    @pl.when(z < depth_z - 1)
    def _():
        pl.semaphore_signal(barrier, inc=1, device_id=(seq, z + 1), device_id_type=MESH)

    pl.semaphore_wait(barrier, 3 + jnp.minimum(z, 1) + jnp.minimum(depth_z - 1 - z, 1))

    def piece(ch, kind, owner, target, first=0, count=None):
        count = depth if count is None else count
        at = buf.at[ch, pl.ds(pl.multiple_of(owner * depth + first, count), count), :]
        return pltpu.make_async_remote_copy(
            src_ref=at,
            dst_ref=at,
            send_sem=w_send.at[ch, kind],
            recv_sem=w_recv.at[ch, kind],
            device_id=(target, z),
            device_id_type=MESH,
        )

    mid = depth // 2

    def outgoing(ch, kind):
        places = (
            (seq, xn),
            (seq, yn),
            (seq, sib),
            (xn, yn, 0, mid),
            (yn, xn, mid, mid),
            (xn, sib),
            (yn, sib),
            (diag, sib),
        )
        return piece(ch, kind, *places[kind])

    def incoming(ch, kind):
        places = (
            (xn, xn),
            (yn, yn),
            (sib, sib),
            (diag, yn, 0, mid),
            (diag, xn, mid, mid),
            (x_sib, sib),
            (y_sib, sib),
            (diag_sib, sib),
        )
        return piece(ch, kind, *places[kind])

    def send_own(ch):
        for kind in (0, 1, 2):
            outgoing(ch, kind).start()

    def pass_near(ch):
        incoming(ch, 0).wait_recv()
        outgoing(ch, 3).start()
        outgoing(ch, 5).start()
        incoming(ch, 1).wait_recv()
        outgoing(ch, 4).start()
        outgoing(ch, 6).start()

    def pass_far(ch):
        incoming(ch, 3).wait_recv()
        incoming(ch, 4).wait_recv()
        outgoing(ch, 7).start()

    def complete(ch):
        for kind in (2, 5, 6, 7):
            incoming(ch, kind).wait_recv()

    def token_copy(way, hop, p, owner):
        at = tok.at[owner, pl.ds(pl.multiple_of(p * part, part), part), :]
        target = z + 1 if way == 0 else z - 1
        return pltpu.make_async_remote_copy(
            src_ref=at,
            dst_ref=at,
            send_sem=t_send.at[way, hop, p],
            recv_sem=t_recv.at[way, hop, p],
            device_id=(seq, target),
            device_id_type=MESH,
        )

    def token_step(t):
        hop, p = t // PARTS, t % PARTS

        @pl.when(z - 1 - hop >= 0)
        def _():
            token_copy(0, hop, p, z - 1 - hop).wait_recv()

            @pl.when(z < depth_z - 1)
            def _():
                token_copy(0, hop + 1, p, z - 1 - hop).start()

        @pl.when(z + 1 + hop < depth_z)
        def _():
            token_copy(1, hop, p, z + 1 + hop).wait_recv()

            @pl.when(z > 0)
            def _():
                token_copy(1, hop + 1, p, z + 1 + hop).start()

    own_copies[0].wait()
    send_own(0)
    tok_copy.wait()

    @pl.loop(0, PARTS)
    def _(p):
        @pl.when(z < depth_z - 1)
        def _():
            token_copy(0, 0, p, z).start()

        @pl.when(z > 0)
        def _():
            token_copy(1, 0, p, z).start()

    for ch in range(1, chunks):
        own_copies[ch].wait()
    for ch in range(1, AHEAD):
        send_own(ch)

    def convert(k):
        step = 32

        @pl.loop(0, rows // step)
        def _(r):
            at = pl.ds(pl.multiple_of(r * step, step), step)
            v = tok[k, at, :].astype(jnp.float32)
            scaled[k, at, :] = (v * norm_gain[k]).astype(jnp.bfloat16)
            v = v * v
            total = squares[at, :]
            for f in range(shard // LANES):
                total = total + v[:, f * LANES : (f + 1) * LANES]
            squares[at, :] = total

    def find_scale():
        mean = jnp.sum(squares[...], axis=1, keepdims=True) / (depth_z * shard)
        row_scale[...] = jnp.broadcast_to(lax.rsqrt(mean + 1e-05), (rows, GROUP))

    def accumulate(ch, k):
        at = pl.ds(pl.multiple_of(k * shard, shard), shard)
        acc[ch] += dot(scaled[k], buf[ch, at, :])

    def finish(ch):
        proj[ch] = (acc[ch] * row_scale[...]).astype(jnp.bfloat16)

        @pl.when((ch % 2 == 1) & (ch < early))
        def _():
            both = dot(proj[ch - 1], proj[ch], ((0,), (0,)))
            for e in range(per):
                st = both[e * size : (e + 1) * size, e * size : (e + 1) * size]
                state_out[ch // 2 * per + e] = st.astype(jnp.bfloat16)

    def begin(ch, first, last):
        complete(ch)
        acc[ch] = jnp.zeros((rows, GROUP), jnp.float32)

        @pl.loop(first, last)
        def _(k):
            accumulate(ch, k)

    def project(ch):
        begin(ch, 0, depth_z)
        finish(ch)

    mine = pl.ds(c * half, half)
    theirs = pl.ds((1 - c) * half, half)

    def state_copy(k, source, target_ref, target):
        return pltpu.make_async_remote_copy(
            src_ref=source,
            dst_ref=target_ref,
            send_sem=s_send.at[k],
            recv_sem=s_recv.at[k],
            device_id=(target, z),
            device_id_type=MESH,
        )

    to_sib = state_copy(0, state_out, state_sib, sib)
    to_x = state_copy(1, sum_out.at[0], sum_in.at[0, mine], xn)
    x_to_sib = state_copy(2, sum_in.at[0, mine], sum_in.at[0, mine], sib)
    to_y = state_copy(3, sum_out.at[1], sum_in.at[1, mine], yn)
    y_to_sib = state_copy(4, sum_in.at[1, mine], sum_in.at[1, mine], sib)
    x_from_sib = state_copy(2, sum_in.at[0, theirs], sum_in.at[0, theirs], sib)
    y_from_sib = state_copy(4, sum_in.at[1, theirs], sum_in.at[1, theirs], sib)

    final_copy = pltpu.make_async_copy(final, final_out, o_sem.at[groups])

    def slab_copy(g):
        cols = pl.ds(g * GROUP, GROUP)
        return pltpu.make_async_copy(attended.at[:, cols], attended_out.at[:, cols], o_sem.at[g])

    def wide(v):
        return v.astype(jnp.float32)

    def state_one():
        to_sib.start()

    def state_two():
        to_sib.wait_recv()
        sum_out[0] = (wide(state_out[mine]) + wide(state_sib[mine])).astype(jnp.bfloat16)
        to_x.start()

    def state_three():
        to_x.wait_recv()
        x_to_sib.start()
        sum_out[1] = (wide(sum_out[0]) + wide(sum_in[0, mine])).astype(jnp.bfloat16)
        to_y.start()

    def state_four():
        to_y.wait_recv()
        y_to_sib.start()

    def state_five():
        x_from_sib.wait_recv()
        y_from_sib.wait_recv()
        on_c = c.astype(jnp.float32)
        on_x = x.astype(jnp.float32)
        on_y = y.astype(jnp.float32)
        for h in range(heads):
            near = wide(state_sib[h])
            chip = (wide(state_out[h]) + near).astype(jnp.bfloat16)
            beside = wide(sum_in[0, h])
            row = (wide(chip) + beside).astype(jnp.bfloat16)
            far = wide(sum_in[1, h])
            start = carried[h]
            before = near * on_c + beside * on_x + far * on_y
            prior[h] = (start + before).astype(jnp.bfloat16)
            final[h] = start + (wide(row) + far)
        final_copy.start()

    top = rows // 2

    def attend(g):
        at = lax.broadcasted_iota(jnp.int32, (top, top), 0)
        of = lax.broadcasted_iota(jnp.int32, (top, top), 1)
        causal = of <= at

        def masked(s):
            return jnp.where(causal, s, 0.0).astype(jnp.bfloat16)

        for e in range(per):
            cols = slice(e * size, (e + 1) * size)
            h = g * per + e
            start = prior[h]
            q0, q1 = proj[early + g, :top, cols], proj[early + g, top:, cols]
            k0, k1 = proj[2 * g, :top, cols], proj[2 * g, top:, cols]
            v0, v1 = proj[2 * g + 1, :top, cols], proj[2 * g + 1, top:, cols]
            across = ((1,), (1,))
            raw0 = dot(q0, start) + dot(masked(dot(q0, k0, across)), v0)
            raw1 = (
                dot(q1, start)
                + dot(dot(q1, k0, across).astype(jnp.bfloat16), v0)
                + dot(masked(dot(q1, k1, across)), v1)
            )
            gain = out_gain[:, h * size : (h + 1) * size]
            for first, raw in ((0, raw0), (top, raw1)):
                scale = lax.rsqrt(jnp.mean(raw * raw, axis=1, keepdims=True) + 1e-06)
                attended[first : first + top, h * size : (h + 1) * size] = (
                    raw * scale * gain
                ).astype(jnp.bfloat16)
        slab_copy(g).start()

    steps = hops * PARTS

    squares[...] = jnp.zeros_like(squares)
    convert(z)

    @pl.loop(0, early)
    def _(i):
        @pl.when(i + AHEAD <= early)
        def _():
            send_own(i + AHEAD)

        pass_near(i)

        @pl.when(i >= LAG)
        def _():
            pass_far(i - LAG)

        first = jnp.minimum(i * steps // early, steps)
        last = jnp.minimum((i + 1) * steps // early, steps)

        @pl.loop(first, last)
        def _(t):
            token_step(t)

        level = last // PARTS
        now = i - LAG - 1

        @pl.when(level > first // PARTS)
        def _():
            for k in (z - level, z + level):

                @pl.when((k >= 0) & (k < depth_z))
                def _(k=k):
                    convert(k)

                    @pl.loop(0, now)
                    def _(ch):
                        accumulate(ch, k)

            @pl.when(level == hops)
            def _():
                find_scale()

                @pl.loop(0, now)
                def _(ch):
                    finish(ch)

        @pl.when(now >= 0)
        def _():
            begin(now, jnp.maximum(z - level, 0), jnp.minimum(z + level + 1, depth_z))

            @pl.when(level == hops)
            def _():
                finish(now)

    send_own(early + 1)
    pass_near(early)
    for ch in range(early - LAG, early):
        pass_far(ch)

    @pl.loop(early - LAG - 1, early)
    def _(ch):
        project(ch)

    state_one()
    state_two()
    done = 0
    for g in range(1, groups):
        i = early + g
        if i + 1 < chunks:
            send_own(i + 1)
        pass_near(i)
        pass_far(i - 1)
        project(i - 1)
        if g == 1:
            state_three()
        if g == 2:
            state_four()
            state_five()
        if i + 1 == chunks:
            pass_far(i)
        if g >= 2:
            for k in range(done, g):
                attend(k)
            done = g
    project(chunks - 1)
    attend(groups - 1)

    @pl.loop(0, chunks)
    def _(ch):
        for kind in range(8):
            outgoing(ch, kind).wait_send()

    @pl.loop(0, steps)
    def _(t):
        hop, p = t // PARTS, t % PARTS

        @pl.when((z < depth_z - 1) & (z - hop >= 0))
        def _():
            token_copy(0, hop, p, z - hop).wait_send()

        @pl.when((z > 0) & (z + hop < depth_z))
        def _():
            token_copy(1, hop, p, z + hop).wait_send()

    for copy in (to_sib, to_x, x_to_sib, to_y, y_to_sib):
        copy.wait_send()
    for g in range(groups):
        slab_copy(g).wait()
    final_copy.wait()


def settle(attended, final, attended_out, final_out, sems):
    rows = attended.shape[0] // PARTS
    heads = final.shape[0] // PARTS
    copies = []
    for p in range(PARTS):
        at = pl.ds(p * rows, rows)
        copies.append(pltpu.make_async_copy(attended.at[at], attended_out.at[at], sems.at[0, p]))
        at = pl.ds(p * heads, heads)
        copies.append(pltpu.make_async_copy(final.at[at], final_out.at[at], sems.at[1, p]))
    for copy in copies:
        copy.start()
    for copy in copies:
        copy.wait()


def fused(depth_z, tokens, norm_gain, w_query, w_key, w_value, out_gain, carried):
    rows, shard = tokens.shape
    depth, width = w_query.shape
    features = norm_gain.shape[0]
    heads, size = carried.shape[0], carried.shape[1]
    chunks = 3 * (width // GROUP)
    any_spec = pl.BlockSpec(memory_space=pl.ANY)
    vmem_spec = pl.BlockSpec(memory_space=pltpu.VMEM)
    dma = pltpu.SemaphoreType.DMA
    shapes = (
        jax.ShapeDtypeStruct((rows, width), jnp.bfloat16),
        jax.ShapeDtypeStruct(carried.shape, jnp.float32),
    )
    results = pl.pallas_call(
        functools.partial(kernel, depth_z),
        out_shape=shapes,
        in_specs=[any_spec, vmem_spec, any_spec, any_spec, any_spec, vmem_spec, vmem_spec],
        out_specs=(any_spec, any_spec),
        scratch_shapes=[
            pltpu.VMEM((depth_z, rows, shard), jnp.bfloat16),
            pltpu.VMEM((depth_z, rows, shard), jnp.bfloat16),
            pltpu.VMEM((rows, LANES), jnp.float32),
            pltpu.VMEM((rows, GROUP), jnp.float32),
            pltpu.VMEM((chunks, features, GROUP), jnp.bfloat16),
            pltpu.VMEM((chunks, rows, GROUP), jnp.float32),
            pltpu.VMEM((chunks, rows, GROUP), jnp.bfloat16),
            pltpu.VMEM((heads, size, size), jnp.bfloat16),
            pltpu.VMEM((heads, size, size), jnp.bfloat16),
            pltpu.VMEM((2, heads // 2, size, size), jnp.bfloat16),
            pltpu.VMEM((2, heads, size, size), jnp.bfloat16),
            pltpu.VMEM((heads, size, size), jnp.bfloat16),
            dma((chunks + 1,)),
            dma((chunks, 8)),
            dma((chunks, 8)),
            dma((2, depth_z, PARTS)),
            dma((2, depth_z, PARTS)),
            dma((5,)),
            dma((5,)),
            pltpu.VMEM((rows, width), jnp.bfloat16),
            pltpu.VMEM(carried.shape, jnp.float32),
            dma((width // GROUP + 1,)),
        ],
        compiler_params=pltpu.CompilerParams(
            collective_id=0, has_side_effects=True, vmem_limit_bytes=56 * 1024 * 1024
        ),
        cost_estimate=pl.CostEstimate(
            flops=6 * rows * features * width, bytes_accessed=8 * depth * width, transcendentals=0
        ),
    )(tokens, norm_gain.reshape(depth_z, 1, shard), w_query, w_key, w_value, out_gain[None], carried)
    return pl.pallas_call(
        settle,
        out_shape=shapes,
        in_specs=[any_spec, any_spec],
        out_specs=(any_spec, any_spec),
        scratch_shapes=[dma((2, PARTS))],
    )(*results)


def solution(mesh):
    square = mesh.shape["seq"] == 8

    def local(tokens, *rest):
        if square and tokens.shape[0] == BLOCK:
            return fused(mesh.shape["tensor"], tokens, *rest)
        return shards(tokens, *rest)

    return jax.shard_map(
        local,
        mesh=mesh,
        in_specs=(
            P("seq", "tensor"),
            P(),
            P("seq", "tensor"),
            P("seq", "tensor"),
            P("seq", "tensor"),
            P("tensor"),
            P("tensor", None, None),
        ),
        out_specs=(P("seq", "tensor"), P("tensor", None, None)),
        check_vma=False,
    )
```

```python
import functools

import jax
import jax.numpy as jnp
from jax import lax
from jax.experimental import pallas as pl
from jax.experimental.pallas import tpu as pltpu
from jax.sharding import PartitionSpec as P

BLOCK = 512
MESH = pl.DeviceIdType.MESH
GROUP = 256
PARTS = 4
AHEAD = 2
LAG = 1
LANES = 128


def add_rows(normed, pieces):
    return tuple((jnp.dot(normed, piece, preferred_element_type=jnp.float32) for piece in pieces))


def shards(tokens, norm_gain, w_query, w_key, w_value, out_gain, carried):
    whole = lax.all_gather(tokens, "tensor", axis=1, tiled=True)
    xf = whole.astype(jnp.float32)
    normed = (xf * lax.rsqrt(jnp.mean(xf * xf, axis=1, keepdims=True) + 1e-05) * norm_gain).astype(
        jnp.bfloat16
    )
    rows = normed.shape[0]
    width = w_query.shape[1]
    size = carried.shape[1]
    heads = width // size
    qsum, ksum, vsum = add_rows(
        normed,
        (
            lax.all_gather(w_query, "seq", axis=0, tiled=True),
            lax.all_gather(w_key, "seq", axis=0, tiled=True),
            lax.all_gather(w_value, "seq", axis=0, tiled=True),
        ),
    )
    blocks = rows // BLOCK
    query = qsum.astype(jnp.bfloat16).reshape(blocks, BLOCK, heads, size)
    key = ksum.astype(jnp.bfloat16).reshape(blocks, BLOCK, heads, size)
    value = vsum.astype(jnp.bfloat16).reshape(blocks, BLOCK, heads, size)
    block_state = jnp.einsum("nthd,nthe->nhde", key, value, preferred_element_type=jnp.float32)
    local_total = jnp.sum(block_state, axis=0)
    zero_state = jnp.zeros_like(local_total)
    mine = lax.axis_index("seq")
    piece = lax.all_gather(
        local_total[None].astype(jnp.bfloat16), "seq", axis=0, tiled=True
    ).astype(jnp.float32)
    where = jnp.arange(piece.shape[0], dtype=jnp.int32)
    keep = (where < mine).astype(jnp.float32)
    before = zero_state + jnp.sum(keep[:, None, None, None] * piece, axis=0)
    total = zero_state + jnp.sum(piece, axis=0)
    start_state = carried + before
    running = jnp.cumsum(block_state, axis=0) - block_state
    priors = start_state[None] + running
    inter = jnp.einsum(
        "nthd,nhde->nthe", query.astype(jnp.float32), priors, precision=lax.Precision.HIGHEST
    )
    causal = jnp.tril(jnp.ones((BLOCK, BLOCK), jnp.float32))
    scores = jnp.einsum("nthd,nshd->nhts", query, key, preferred_element_type=jnp.float32)
    weights = (scores * causal).astype(jnp.bfloat16)
    intra = jnp.einsum("nhts,nshe->nthe", weights, value, preferred_element_type=jnp.float32)
    raw = inter + intra
    normal = (
        raw
        * lax.rsqrt(jnp.mean(raw * raw, axis=3, keepdims=True) + 1e-06)
        * out_gain.reshape(heads, size)
    )
    attended = normal.astype(jnp.bfloat16).reshape(rows, width)
    return (attended, carried + total)


def dot(a, b, dims=((1,), (0,))):
    return lax.dot_general(a, b, (dims, ((), ())), preferred_element_type=jnp.float32)


def kernel(
    depth_z,
    tokens,
    norm_gain,
    w_query,
    w_key,
    w_value,
    out_gain,
    carried,
    attended_out,
    final_out,
    tok,
    scaled,
    squares,
    row_scale,
    buf,
    acc,
    proj,
    state_out,
    state_sib,
    sum_out,
    sum_in,
    prior,
    local_sem,
    w_send,
    w_recv,
    t_send,
    t_recv,
    s_send,
    s_recv,
    attended,
    final,
    o_sem,
):
    rows, shard = tokens.shape
    depth = w_query.shape[0]
    groups = w_query.shape[1] // GROUP
    size = carried.shape[1]
    heads = carried.shape[0]
    per = GROUP // size
    half = heads // 2
    early = 2 * groups
    chunks = 3 * groups
    part = rows // PARTS
    hops = depth_z - 1

    seq = lax.axis_index("seq")
    z = lax.axis_index("tensor")
    c = seq % 2
    x = (seq // 2) % 2
    y = seq // 4
    sib = y * 4 + x * 2 + (1 - c)
    xn = y * 4 + (1 - x) * 2 + c
    yn = (1 - y) * 4 + x * 2 + c
    diag = (1 - y) * 4 + (1 - x) * 2 + c
    x_sib = y * 4 + (1 - x) * 2 + (1 - c)
    y_sib = (1 - y) * 4 + x * 2 + (1 - c)
    diag_sib = (1 - y) * 4 + (1 - x) * 2 + (1 - c)

    tok_copy = pltpu.make_async_copy(tokens, tok.at[z], local_sem.at[chunks])
    tok_copy.start()
    own_copies = []
    for ch in range(chunks):
        if ch < early:
            ref, g = (w_key, w_value)[ch % 2], ch // 2
        else:
            ref, g = w_query, ch - early
        copy = pltpu.make_async_copy(
            ref.at[:, pl.ds(g * GROUP, GROUP)],
            buf.at[ch, pl.ds(pl.multiple_of(seq * depth, depth), depth), :],
            local_sem.at[ch],
        )
        copy.start()
        own_copies.append(copy)

    barrier = pltpu.get_barrier_semaphore()
    for other in (sib, xn, yn):
        pl.semaphore_signal(barrier, inc=1, device_id=(other, z), device_id_type=MESH)

    @pl.when(z > 0)
    def _():
        pl.semaphore_signal(barrier, inc=1, device_id=(seq, z - 1), device_id_type=MESH)

    @pl.when(z < depth_z - 1)
    def _():
        pl.semaphore_signal(barrier, inc=1, device_id=(seq, z + 1), device_id_type=MESH)

    pl.semaphore_wait(barrier, 3 + jnp.minimum(z, 1) + jnp.minimum(depth_z - 1 - z, 1))

    def piece(ch, kind, owner, target, first=0, count=None):
        count = depth if count is None else count
        at = buf.at[ch, pl.ds(pl.multiple_of(owner * depth + first, count), count), :]
        return pltpu.make_async_remote_copy(
            src_ref=at,
            dst_ref=at,
            send_sem=w_send.at[ch, kind],
            recv_sem=w_recv.at[ch, kind],
            device_id=(target, z),
            device_id_type=MESH,
        )

    mid = depth // 2

    def outgoing(ch, kind):
        places = (
            (seq, xn),
            (seq, yn),
            (seq, sib),
            (xn, yn, 0, mid),
            (yn, xn, mid, mid),
            (xn, sib),
            (yn, sib),
            (diag, sib),
        )
        return piece(ch, kind, *places[kind])

    def incoming(ch, kind):
        places = (
            (xn, xn),
            (yn, yn),
            (sib, sib),
            (diag, yn, 0, mid),
            (diag, xn, mid, mid),
            (x_sib, sib),
            (y_sib, sib),
            (diag_sib, sib),
        )
        return piece(ch, kind, *places[kind])

    def send_own(ch):
        for kind in (0, 1, 2):
            outgoing(ch, kind).start()

    def pass_near(ch):
        incoming(ch, 0).wait_recv()
        outgoing(ch, 3).start()
        outgoing(ch, 5).start()
        incoming(ch, 1).wait_recv()
        outgoing(ch, 4).start()
        outgoing(ch, 6).start()

    def pass_far(ch):
        incoming(ch, 3).wait_recv()
        incoming(ch, 4).wait_recv()
        outgoing(ch, 7).start()

    def complete(ch):
        for kind in (2, 5, 6, 7):
            incoming(ch, kind).wait_recv()

    def token_copy(way, hop, p, owner):
        at = tok.at[owner, pl.ds(pl.multiple_of(p * part, part), part), :]
        target = z + 1 if way == 0 else z - 1
        return pltpu.make_async_remote_copy(
            src_ref=at,
            dst_ref=at,
            send_sem=t_send.at[way, hop, p],
            recv_sem=t_recv.at[way, hop, p],
            device_id=(seq, target),
            device_id_type=MESH,
        )

    def token_step(t):
        hop, p = t // PARTS, t % PARTS

        @pl.when(z - 1 - hop >= 0)
        def _():
            token_copy(0, hop, p, z - 1 - hop).wait_recv()

            @pl.when(z < depth_z - 1)
            def _():
                token_copy(0, hop + 1, p, z - 1 - hop).start()

        @pl.when(z + 1 + hop < depth_z)
        def _():
            token_copy(1, hop, p, z + 1 + hop).wait_recv()

            @pl.when(z > 0)
            def _():
                token_copy(1, hop + 1, p, z + 1 + hop).start()

    own_copies[0].wait()
    send_own(0)
    tok_copy.wait()

    @pl.loop(0, PARTS)
    def _(p):
        @pl.when(z < depth_z - 1)
        def _():
            token_copy(0, 0, p, z).start()

        @pl.when(z > 0)
        def _():
            token_copy(1, 0, p, z).start()

    for ch in range(1, chunks):
        own_copies[ch].wait()
    for ch in range(1, AHEAD):
        send_own(ch)

    def convert(k):
        step = 32

        @pl.loop(0, rows // step)
        def _(r):
            at = pl.ds(pl.multiple_of(r * step, step), step)
            v = tok[k, at, :].astype(jnp.float32)
            scaled[k, at, :] = (v * norm_gain[k]).astype(jnp.bfloat16)
            v = v * v
            total = squares[at, :]
            for f in range(shard // LANES):
                total = total + v[:, f * LANES : (f + 1) * LANES]
            squares[at, :] = total

    def find_scale():
        mean = jnp.sum(squares[...], axis=1, keepdims=True) / (depth_z * shard)
        row_scale[...] = jnp.broadcast_to(lax.rsqrt(mean + 1e-05), (rows, GROUP))

    def accumulate(ch, k):
        at = pl.ds(pl.multiple_of(k * shard, shard), shard)
        acc[ch] += dot(scaled[k], buf[ch, at, :])

    def finish(ch):
        proj[ch] = (acc[ch] * row_scale[...]).astype(jnp.bfloat16)

        @pl.when((ch % 2 == 1) & (ch < early))
        def _():
            both = dot(proj[ch - 1], proj[ch], ((0,), (0,)))
            for e in range(per):
                st = both[e * size : (e + 1) * size, e * size : (e + 1) * size]
                state_out[ch // 2 * per + e] = st.astype(jnp.bfloat16)

    def begin(ch, first, last):
        complete(ch)
        acc[ch] = jnp.zeros((rows, GROUP), jnp.float32)

        @pl.loop(first, last)
        def _(k):
            accumulate(ch, k)

    def project(ch):
        begin(ch, 0, depth_z)
        finish(ch)

    mine = pl.ds(c * half, half)
    theirs = pl.ds((1 - c) * half, half)

    def state_copy(k, source, target_ref, target):
        return pltpu.make_async_remote_copy(
            src_ref=source,
            dst_ref=target_ref,
            send_sem=s_send.at[k],
            recv_sem=s_recv.at[k],
            device_id=(target, z),
            device_id_type=MESH,
        )

    to_sib = state_copy(0, state_out, state_sib, sib)
    to_x = state_copy(1, sum_out.at[0], sum_in.at[0, mine], xn)
    x_to_sib = state_copy(2, sum_in.at[0, mine], sum_in.at[0, mine], sib)
    to_y = state_copy(3, sum_out.at[1], sum_in.at[1, mine], yn)
    y_to_sib = state_copy(4, sum_in.at[1, mine], sum_in.at[1, mine], sib)
    x_from_sib = state_copy(2, sum_in.at[0, theirs], sum_in.at[0, theirs], sib)
    y_from_sib = state_copy(4, sum_in.at[1, theirs], sum_in.at[1, theirs], sib)

    final_copy = pltpu.make_async_copy(final, final_out, o_sem.at[groups])

    def slab_copy(g):
        cols = pl.ds(g * GROUP, GROUP)
        return pltpu.make_async_copy(attended.at[:, cols], attended_out.at[:, cols], o_sem.at[g])

    def wide(v):
        return v.astype(jnp.float32)

    def state_one():
        to_sib.start()

    def state_two():
        to_sib.wait_recv()
        sum_out[0] = (wide(state_out[mine]) + wide(state_sib[mine])).astype(jnp.bfloat16)
        to_x.start()

    def state_three():
        to_x.wait_recv()
        x_to_sib.start()
        sum_out[1] = (wide(sum_out[0]) + wide(sum_in[0, mine])).astype(jnp.bfloat16)
        to_y.start()

    def state_four():
        to_y.wait_recv()
        y_to_sib.start()

    def state_five():
        x_from_sib.wait_recv()
        y_from_sib.wait_recv()
        on_c = c.astype(jnp.float32)
        on_x = x.astype(jnp.float32)
        on_y = y.astype(jnp.float32)
        for h in range(heads):
            near = wide(state_sib[h])
            chip = (wide(state_out[h]) + near).astype(jnp.bfloat16)
            beside = wide(sum_in[0, h])
            row = (wide(chip) + beside).astype(jnp.bfloat16)
            far = wide(sum_in[1, h])
            start = carried[h]
            before = near * on_c + beside * on_x + far * on_y
            prior[h] = (start + before).astype(jnp.bfloat16)
            final[h] = start + (wide(row) + far)
        final_copy.start()

    top = rows // 2

    def attend(g):
        at = lax.broadcasted_iota(jnp.int32, (top, top), 0)
        of = lax.broadcasted_iota(jnp.int32, (top, top), 1)
        causal = of <= at

        def masked(s):
            return jnp.where(causal, s, 0.0).astype(jnp.bfloat16)

        for e in range(per):
            cols = slice(e * size, (e + 1) * size)
            h = g * per + e
            start = prior[h]
            q0, q1 = proj[early + g, :top, cols], proj[early + g, top:, cols]
            k0, k1 = proj[2 * g, :top, cols], proj[2 * g, top:, cols]
            v0, v1 = proj[2 * g + 1, :top, cols], proj[2 * g + 1, top:, cols]
            across = ((1,), (1,))
            raw0 = dot(q0, start) + dot(masked(dot(q0, k0, across)), v0)
            raw1 = (
                dot(q1, start)
                + dot(dot(q1, k0, across).astype(jnp.bfloat16), v0)
                + dot(masked(dot(q1, k1, across)), v1)
            )
            gain = out_gain[:, h * size : (h + 1) * size]
            for first, raw in ((0, raw0), (top, raw1)):
                scale = lax.rsqrt(jnp.mean(raw * raw, axis=1, keepdims=True) + 1e-06)
                attended[first : first + top, h * size : (h + 1) * size] = (
                    raw * scale * gain
                ).astype(jnp.bfloat16)
        slab_copy(g).start()

    steps = hops * PARTS

    squares[...] = jnp.zeros_like(squares)
    convert(z)

    @pl.loop(0, early)
    def _(i):
        pass_near(i)
        send_own(i + AHEAD)

        @pl.when(i >= LAG)
        def _():
            pass_far(i - LAG)

        first = jnp.minimum(i * steps // early, steps)
        last = jnp.minimum((i + 1) * steps // early, steps)

        @pl.loop(first, last)
        def _(t):
            token_step(t)

        level = last // PARTS
        now = i - LAG - 1

        @pl.when(level > first // PARTS)
        def _():
            for k in (z - level, z + level):

                @pl.when((k >= 0) & (k < depth_z))
                def _(k=k):
                    convert(k)

                    @pl.loop(0, now)
                    def _(ch):
                        accumulate(ch, k)

            @pl.when(level == hops)
            def _():
                find_scale()

                @pl.loop(0, now)
                def _(ch):
                    finish(ch)

        @pl.when(now >= 0)
        def _():
            begin(now, jnp.maximum(z - level, 0), jnp.minimum(z + level + 1, depth_z))

            @pl.when(level == hops)
            def _():
                finish(now)

    pass_near(early)
    pass_far(early - 1)

    @pl.loop(early - LAG - 1, early)
    def _(ch):
        project(ch)

    state_one()
    state_two()
    send_own(early + 2)
    for g in range(1, groups - 1):
        i = early + g
        pass_near(i)
        pass_far(i - 1)
        if g == 1:
            state_three()
        if g == groups - 2:
            state_four()
        if i + AHEAD < chunks:
            send_own(i + AHEAD)
        project(i - 1)
    state_five()
    for g in range(groups - 2):
        attend(g)

    last = chunks - 1
    pass_near(last)
    acc[last] = jnp.zeros((rows, GROUP), jnp.float32)
    for kind, owner in ((2, seq), (5, xn), (6, yn)):
        incoming(last, kind).wait_recv()
        accumulate(last, owner // 2)
    pass_far(last - 1)
    project(last - 1)
    pass_far(last)
    attend(groups - 2)
    incoming(last, 7).wait_recv()
    accumulate(last, diag // 2)
    finish(last)
    attend(groups - 1)

    @pl.loop(0, chunks)
    def _(ch):
        for kind in range(8):
            outgoing(ch, kind).wait_send()

    @pl.loop(0, steps)
    def _(t):
        hop, p = t // PARTS, t % PARTS

        @pl.when((z < depth_z - 1) & (z - hop >= 0))
        def _():
            token_copy(0, hop, p, z - hop).wait_send()

        @pl.when((z > 0) & (z + hop < depth_z))
        def _():
            token_copy(1, hop, p, z + hop).wait_send()

    for copy in (to_sib, to_x, x_to_sib, to_y, y_to_sib):
        copy.wait_send()
    for g in range(groups):
        slab_copy(g).wait()
    final_copy.wait()


def settle(attended, final, attended_out, final_out, held, held_final, sem_in, sem_out):
    rows = attended.shape[0] // PARTS
    heads = final.shape[0] // PARTS
    comes, goes = [], []
    for p in range(PARTS):
        for k, count, source, here, target in (
            (0, rows, attended, held, attended_out),
            (1, heads, final, held_final, final_out),
        ):
            at = pl.ds(p * count, count)
            comes.append(pltpu.make_async_copy(source.at[at], here.at[at], sem_in.at[k, p]))
            goes.append(pltpu.make_async_copy(here.at[at], target.at[at], sem_out.at[k, p]))
    for copy in comes:
        copy.start()
    for copy, onward in zip(comes, goes):
        copy.wait()
        onward.start()
    for onward in goes:
        onward.wait()


def fused(depth_z, tokens, norm_gain, w_query, w_key, w_value, out_gain, carried):
    rows, shard = tokens.shape
    depth, width = w_query.shape
    features = norm_gain.shape[0]
    heads, size = carried.shape[0], carried.shape[1]
    chunks = 3 * (width // GROUP)
    any_spec = pl.BlockSpec(memory_space=pl.ANY)
    vmem_spec = pl.BlockSpec(memory_space=pltpu.VMEM)
    dma = pltpu.SemaphoreType.DMA
    shapes = (
        jax.ShapeDtypeStruct((rows, width), jnp.bfloat16),
        jax.ShapeDtypeStruct(carried.shape, jnp.float32),
    )
    results = pl.pallas_call(
        functools.partial(kernel, depth_z),
        out_shape=shapes,
        in_specs=[any_spec, vmem_spec, any_spec, any_spec, any_spec, vmem_spec, vmem_spec],
        out_specs=(any_spec, any_spec),
        scratch_shapes=[
            pltpu.VMEM((depth_z, rows, shard), jnp.bfloat16),
            pltpu.VMEM((depth_z, rows, shard), jnp.bfloat16),
            pltpu.VMEM((rows, LANES), jnp.float32),
            pltpu.VMEM((rows, GROUP), jnp.float32),
            pltpu.VMEM((chunks, features, GROUP), jnp.bfloat16),
            pltpu.VMEM((chunks, rows, GROUP), jnp.float32),
            pltpu.VMEM((chunks, rows, GROUP), jnp.bfloat16),
            pltpu.VMEM((heads, size, size), jnp.bfloat16),
            pltpu.VMEM((heads, size, size), jnp.bfloat16),
            pltpu.VMEM((2, heads // 2, size, size), jnp.bfloat16),
            pltpu.VMEM((2, heads, size, size), jnp.bfloat16),
            pltpu.VMEM((heads, size, size), jnp.bfloat16),
            dma((chunks + 1,)),
            dma((chunks, 8)),
            dma((chunks, 8)),
            dma((2, depth_z, PARTS)),
            dma((2, depth_z, PARTS)),
            dma((5,)),
            dma((5,)),
            pltpu.VMEM((rows, width), jnp.bfloat16),
            pltpu.VMEM(carried.shape, jnp.float32),
            dma((width // GROUP + 1,)),
        ],
        compiler_params=pltpu.CompilerParams(
            collective_id=0, has_side_effects=True, vmem_limit_bytes=56 * 1024 * 1024
        ),
        cost_estimate=pl.CostEstimate(
            flops=6 * rows * features * width, bytes_accessed=8 * depth * width, transcendentals=0
        ),
    )(tokens, norm_gain.reshape(depth_z, 1, shard), w_query, w_key, w_value, out_gain[None], carried)
    return pl.pallas_call(
        settle,
        out_shape=shapes,
        in_specs=[any_spec, any_spec],
        out_specs=(any_spec, any_spec),
        scratch_shapes=[
            pltpu.VMEM((rows, width), jnp.bfloat16),
            pltpu.VMEM(carried.shape, jnp.float32),
            dma((2, PARTS)),
            dma((2, PARTS)),
        ],
        compiler_params=pltpu.CompilerParams(vmem_limit_bytes=60 * 1024 * 1024),
    )(*results)


def solution(mesh):
    square = mesh.shape["seq"] == 8 and mesh.shape["tensor"] == 4

    def local(tokens, *rest):
        if square and tokens.shape[0] == BLOCK:
            return fused(mesh.shape["tensor"], tokens, *rest)
        return shards(tokens, *rest)

    return jax.shard_map(
        local,
        mesh=mesh,
        in_specs=(
            P("seq", "tensor"),
            P(),
            P("seq", "tensor"),
            P("seq", "tensor"),
            P("seq", "tensor"),
            P("tensor"),
            P("tensor", None, None),
        ),
        out_specs=(P("seq", "tensor"), P("tensor", None, None)),
        check_vma=False,
    )
```

```python
import functools

import jax
import jax.numpy as jnp
from jax import lax
from jax.experimental import pallas as pl
from jax.experimental.pallas import tpu as pltpu
from jax.sharding import PartitionSpec as P

BLOCK = 512
MESH = pl.DeviceIdType.MESH
GROUP = 256
PARTS = 4
AHEAD = 3
LAG = 2
LANES = 128


def add_rows(normed, pieces):
    return tuple((jnp.dot(normed, piece, preferred_element_type=jnp.float32) for piece in pieces))


def shards(tokens, norm_gain, w_query, w_key, w_value, out_gain, carried):
    whole = lax.all_gather(tokens, "tensor", axis=1, tiled=True)
    xf = whole.astype(jnp.float32)
    normed = (xf * lax.rsqrt(jnp.mean(xf * xf, axis=1, keepdims=True) + 1e-05) * norm_gain).astype(
        jnp.bfloat16
    )
    rows = normed.shape[0]
    width = w_query.shape[1]
    size = carried.shape[1]
    heads = width // size
    qsum, ksum, vsum = add_rows(
        normed,
        (
            lax.all_gather(w_query, "seq", axis=0, tiled=True),
            lax.all_gather(w_key, "seq", axis=0, tiled=True),
            lax.all_gather(w_value, "seq", axis=0, tiled=True),
        ),
    )
    blocks = rows // BLOCK
    query = qsum.astype(jnp.bfloat16).reshape(blocks, BLOCK, heads, size)
    key = ksum.astype(jnp.bfloat16).reshape(blocks, BLOCK, heads, size)
    value = vsum.astype(jnp.bfloat16).reshape(blocks, BLOCK, heads, size)
    block_state = jnp.einsum("nthd,nthe->nhde", key, value, preferred_element_type=jnp.float32)
    local_total = jnp.sum(block_state, axis=0)
    zero_state = jnp.zeros_like(local_total)
    mine = lax.axis_index("seq")
    piece = lax.all_gather(
        local_total[None].astype(jnp.bfloat16), "seq", axis=0, tiled=True
    ).astype(jnp.float32)
    where = jnp.arange(piece.shape[0], dtype=jnp.int32)
    keep = (where < mine).astype(jnp.float32)
    before = zero_state + jnp.sum(keep[:, None, None, None] * piece, axis=0)
    total = zero_state + jnp.sum(piece, axis=0)
    start_state = carried + before
    running = jnp.cumsum(block_state, axis=0) - block_state
    priors = start_state[None] + running
    inter = jnp.einsum(
        "nthd,nhde->nthe", query.astype(jnp.float32), priors, precision=lax.Precision.HIGHEST
    )
    causal = jnp.tril(jnp.ones((BLOCK, BLOCK), jnp.float32))
    scores = jnp.einsum("nthd,nshd->nhts", query, key, preferred_element_type=jnp.float32)
    weights = (scores * causal).astype(jnp.bfloat16)
    intra = jnp.einsum("nhts,nshe->nthe", weights, value, preferred_element_type=jnp.float32)
    raw = inter + intra
    normal = (
        raw
        * lax.rsqrt(jnp.mean(raw * raw, axis=3, keepdims=True) + 1e-06)
        * out_gain.reshape(heads, size)
    )
    attended = normal.astype(jnp.bfloat16).reshape(rows, width)
    return (attended, carried + total)


def dot(a, b, dims=((1,), (0,))):
    return lax.dot_general(a, b, (dims, ((), ())), preferred_element_type=jnp.float32)


def kernel(
    depth_z,
    tokens,
    norm_gain,
    w_query,
    w_key,
    w_value,
    out_gain,
    carried,
    attended_out,
    final_out,
    tok,
    scaled,
    squares,
    row_scale,
    buf,
    acc,
    proj,
    state_out,
    state_sib,
    sum_out,
    sum_in,
    prior,
    local_sem,
    w_send,
    w_recv,
    t_send,
    t_recv,
    s_send,
    s_recv,
    attended,
    final,
    o_sem,
):
    rows, shard = tokens.shape
    depth = w_query.shape[0]
    groups = w_query.shape[1] // GROUP
    size = carried.shape[1]
    heads = carried.shape[0]
    per = GROUP // size
    half = heads // 2
    early = 2 * groups
    chunks = 3 * groups
    part = rows // PARTS
    hops = depth_z - 1

    seq = lax.axis_index("seq")
    z = lax.axis_index("tensor")
    c = seq % 2
    x = (seq // 2) % 2
    y = seq // 4
    sib = y * 4 + x * 2 + (1 - c)
    xn = y * 4 + (1 - x) * 2 + c
    yn = (1 - y) * 4 + x * 2 + c
    diag = (1 - y) * 4 + (1 - x) * 2 + c
    x_sib = y * 4 + (1 - x) * 2 + (1 - c)
    y_sib = (1 - y) * 4 + x * 2 + (1 - c)
    diag_sib = (1 - y) * 4 + (1 - x) * 2 + (1 - c)

    tok_copy = pltpu.make_async_copy(tokens, tok.at[z], local_sem.at[chunks])
    tok_copy.start()
    own_copies = []
    for ch in range(chunks):
        if ch < early:
            ref, g = (w_key, w_value)[ch % 2], ch // 2
        else:
            ref, g = w_query, ch - early
        copy = pltpu.make_async_copy(
            ref.at[:, pl.ds(g * GROUP, GROUP)],
            buf.at[ch, pl.ds(pl.multiple_of(seq * depth, depth), depth), :],
            local_sem.at[ch],
        )
        copy.start()
        own_copies.append(copy)

    barrier = pltpu.get_barrier_semaphore()
    for other in (sib, xn, yn):
        pl.semaphore_signal(barrier, inc=1, device_id=(other, z), device_id_type=MESH)

    @pl.when(z > 0)
    def _():
        pl.semaphore_signal(barrier, inc=1, device_id=(seq, z - 1), device_id_type=MESH)

    @pl.when(z < depth_z - 1)
    def _():
        pl.semaphore_signal(barrier, inc=1, device_id=(seq, z + 1), device_id_type=MESH)

    pl.semaphore_wait(barrier, 3 + jnp.minimum(z, 1) + jnp.minimum(depth_z - 1 - z, 1))

    def piece(ch, kind, owner, target, first=0, count=None):
        count = depth if count is None else count
        at = buf.at[ch, pl.ds(pl.multiple_of(owner * depth + first, count), count), :]
        return pltpu.make_async_remote_copy(
            src_ref=at,
            dst_ref=at,
            send_sem=w_send.at[ch, kind],
            recv_sem=w_recv.at[ch, kind],
            device_id=(target, z),
            device_id_type=MESH,
        )

    mid = depth // 2

    def outgoing(ch, kind):
        places = (
            (seq, xn),
            (seq, yn),
            (seq, sib),
            (xn, yn, 0, mid),
            (yn, xn, mid, mid),
            (xn, sib),
            (yn, sib),
            (diag, sib),
        )
        return piece(ch, kind, *places[kind])

    def incoming(ch, kind):
        places = (
            (xn, xn),
            (yn, yn),
            (sib, sib),
            (diag, yn, 0, mid),
            (diag, xn, mid, mid),
            (x_sib, sib),
            (y_sib, sib),
            (diag_sib, sib),
        )
        return piece(ch, kind, *places[kind])

    def send_own(ch):
        for kind in (0, 1, 2):
            outgoing(ch, kind).start()

    def pass_near(ch):
        incoming(ch, 0).wait_recv()
        outgoing(ch, 3).start()
        outgoing(ch, 5).start()
        incoming(ch, 1).wait_recv()
        outgoing(ch, 4).start()
        outgoing(ch, 6).start()

    def pass_far(ch):
        incoming(ch, 3).wait_recv()
        incoming(ch, 4).wait_recv()
        outgoing(ch, 7).start()

    def complete(ch):
        for kind in (2, 5, 6, 7):
            incoming(ch, kind).wait_recv()

    def token_copy(way, hop, p, owner):
        at = tok.at[owner, pl.ds(pl.multiple_of(p * part, part), part), :]
        target = z + 1 if way == 0 else z - 1
        return pltpu.make_async_remote_copy(
            src_ref=at,
            dst_ref=at,
            send_sem=t_send.at[way, hop, p],
            recv_sem=t_recv.at[way, hop, p],
            device_id=(seq, target),
            device_id_type=MESH,
        )

    def token_step(t):
        hop, p = t // PARTS, t % PARTS

        @pl.when(z - 1 - hop >= 0)
        def _():
            token_copy(0, hop, p, z - 1 - hop).wait_recv()

            @pl.when(z < depth_z - 1)
            def _():
                token_copy(0, hop + 1, p, z - 1 - hop).start()

        @pl.when(z + 1 + hop < depth_z)
        def _():
            token_copy(1, hop, p, z + 1 + hop).wait_recv()

            @pl.when(z > 0)
            def _():
                token_copy(1, hop + 1, p, z + 1 + hop).start()

    own_copies[0].wait()
    send_own(0)
    tok_copy.wait()

    @pl.loop(0, PARTS)
    def _(p):
        @pl.when(z < depth_z - 1)
        def _():
            token_copy(0, 0, p, z).start()

        @pl.when(z > 0)
        def _():
            token_copy(1, 0, p, z).start()

    for ch in range(1, chunks):
        own_copies[ch].wait()
    for ch in range(1, AHEAD):
        send_own(ch)

    def convert(k):
        step = 32

        @pl.loop(0, rows // step)
        def _(r):
            at = pl.ds(pl.multiple_of(r * step, step), step)
            v = tok[k, at, :].astype(jnp.float32)
            scaled[k, at, :] = (v * norm_gain[k]).astype(jnp.bfloat16)
            v = v * v
            total = squares[at, :]
            for f in range(shard // LANES):
                total = total + v[:, f * LANES : (f + 1) * LANES]
            squares[at, :] = total

    def find_scale():
        mean = jnp.sum(squares[...], axis=1, keepdims=True) / (depth_z * shard)
        row_scale[...] = jnp.broadcast_to(lax.rsqrt(mean + 1e-05), (rows, GROUP))

    def accumulate(ch, k):
        at = pl.ds(pl.multiple_of(k * shard, shard), shard)
        acc[ch] += dot(scaled[k], buf[ch, at, :])

    def finish(ch):
        proj[ch] = (acc[ch] * row_scale[...]).astype(jnp.bfloat16)

        @pl.when((ch % 2 == 1) & (ch < early))
        def _():
            both = dot(proj[ch - 1], proj[ch], ((0,), (0,)))
            for e in range(per):
                st = both[e * size : (e + 1) * size, e * size : (e + 1) * size]
                state_out[ch // 2 * per + e] = st.astype(jnp.bfloat16)

    def begin(ch, first, last):
        complete(ch)
        acc[ch] = jnp.zeros((rows, GROUP), jnp.float32)

        @pl.loop(first, last)
        def _(k):
            accumulate(ch, k)

    def project(ch):
        begin(ch, 0, depth_z)
        finish(ch)

    mine = pl.ds(c * half, half)
    theirs = pl.ds((1 - c) * half, half)

    def state_copy(k, source, target_ref, target):
        return pltpu.make_async_remote_copy(
            src_ref=source,
            dst_ref=target_ref,
            send_sem=s_send.at[k],
            recv_sem=s_recv.at[k],
            device_id=(target, z),
            device_id_type=MESH,
        )

    to_sib = state_copy(0, state_out, state_sib, sib)
    to_x = state_copy(1, sum_out.at[0], sum_in.at[0, mine], xn)
    x_to_sib = state_copy(2, sum_in.at[0, mine], sum_in.at[0, mine], sib)
    to_y = state_copy(3, sum_out.at[1], sum_in.at[1, mine], yn)
    y_to_sib = state_copy(4, sum_in.at[1, mine], sum_in.at[1, mine], sib)
    x_from_sib = state_copy(2, sum_in.at[0, theirs], sum_in.at[0, theirs], sib)
    y_from_sib = state_copy(4, sum_in.at[1, theirs], sum_in.at[1, theirs], sib)

    final_copy = pltpu.make_async_copy(final, final_out, o_sem.at[groups])

    def slab_copy(g):
        cols = pl.ds(g * GROUP, GROUP)
        return pltpu.make_async_copy(attended.at[:, cols], attended_out.at[:, cols], o_sem.at[g])

    def wide(v):
        return v.astype(jnp.float32)

    def state_one():
        to_sib.start()

    def state_two():
        to_sib.wait_recv()
        sum_out[0] = (wide(state_out[mine]) + wide(state_sib[mine])).astype(jnp.bfloat16)
        to_x.start()

    def state_three():
        to_x.wait_recv()
        x_to_sib.start()
        sum_out[1] = (wide(sum_out[0]) + wide(sum_in[0, mine])).astype(jnp.bfloat16)
        to_y.start()

    def state_four():
        to_y.wait_recv()
        y_to_sib.start()

    def state_five():
        x_from_sib.wait_recv()
        y_from_sib.wait_recv()
        on_c = c.astype(jnp.float32)
        on_x = x.astype(jnp.float32)
        on_y = y.astype(jnp.float32)
        for h in range(heads):
            near = wide(state_sib[h])
            chip = (wide(state_out[h]) + near).astype(jnp.bfloat16)
            beside = wide(sum_in[0, h])
            row = (wide(chip) + beside).astype(jnp.bfloat16)
            far = wide(sum_in[1, h])
            start = carried[h]
            before = near * on_c + beside * on_x + far * on_y
            prior[h] = (start + before).astype(jnp.bfloat16)
            final[h] = start + (wide(row) + far)
        final_copy.start()

    top = rows // 2

    def attend(g):
        at = lax.broadcasted_iota(jnp.int32, (top, top), 0)
        of = lax.broadcasted_iota(jnp.int32, (top, top), 1)
        causal = of <= at

        def masked(s):
            return jnp.where(causal, s, 0.0).astype(jnp.bfloat16)

        for e in range(per):
            cols = slice(e * size, (e + 1) * size)
            h = g * per + e
            start = prior[h]
            q0, q1 = proj[early + g, :top, cols], proj[early + g, top:, cols]
            k0, k1 = proj[2 * g, :top, cols], proj[2 * g, top:, cols]
            v0, v1 = proj[2 * g + 1, :top, cols], proj[2 * g + 1, top:, cols]
            across = ((1,), (1,))
            raw0 = dot(q0, start) + dot(masked(dot(q0, k0, across)), v0)
            raw1 = (
                dot(q1, start)
                + dot(dot(q1, k0, across).astype(jnp.bfloat16), v0)
                + dot(masked(dot(q1, k1, across)), v1)
            )
            gain = out_gain[:, h * size : (h + 1) * size]
            for first, raw in ((0, raw0), (top, raw1)):
                scale = lax.rsqrt(jnp.mean(raw * raw, axis=1, keepdims=True) + 1e-06)
                attended[first : first + top, h * size : (h + 1) * size] = (
                    raw * scale * gain
                ).astype(jnp.bfloat16)
        slab_copy(g).start()

    steps = hops * PARTS

    squares[...] = jnp.zeros_like(squares)
    convert(z)

    @pl.loop(0, early)
    def _(i):
        pass_near(i)

        @pl.when(i + AHEAD <= early)
        def _():
            send_own(i + AHEAD)

        @pl.when(i == early - 1)
        def _():
            send_own(early + 1)

        @pl.when(i >= LAG)
        def _():
            pass_far(i - LAG)

        first = jnp.minimum(i * steps // early, steps)
        last = jnp.minimum((i + 1) * steps // early, steps)

        @pl.loop(first, last)
        def _(t):
            token_step(t)

        level = last // PARTS
        now = i - LAG - 1

        @pl.when(level > first // PARTS)
        def _():
            for k in (z - level, z + level):

                @pl.when((k >= 0) & (k < depth_z))
                def _(k=k):
                    convert(k)

                    @pl.loop(0, now)
                    def _(ch):
                        accumulate(ch, k)

            @pl.when(level == hops)
            def _():
                find_scale()

                @pl.loop(0, now)
                def _(ch):
                    finish(ch)

        @pl.when(now >= 0)
        def _():
            begin(now, jnp.maximum(z - level, 0), jnp.minimum(z + level + 1, depth_z))

            @pl.when(level == hops)
            def _():
                finish(now)

    pass_near(early)
    pass_far(early - 2)
    project(early - 3)
    pass_far(early - 1)

    @pl.loop(early - 2, early)
    def _(ch):
        project(ch)

    state_one()
    state_two()
    send_own(early + 2)
    for g in range(1, groups - 1):
        i = early + g
        pass_near(i)
        pass_far(i - 1)
        if g == 1:
            state_three()
        if g == groups - 2:
            state_four()
        if i + 2 < chunks:
            send_own(i + 2)
        project(i - 1)
    state_five()
    for g in range(groups - 2):
        attend(g)

    last = chunks - 1
    pass_near(last)
    acc[last] = jnp.zeros((rows, GROUP), jnp.float32)
    for kind, owner in ((2, seq), (5, xn), (6, yn)):
        incoming(last, kind).wait_recv()
        accumulate(last, owner // 2)
    pass_far(last - 1)
    project(last - 1)
    pass_far(last)
    attend(groups - 2)
    incoming(last, 7).wait_recv()
    accumulate(last, diag // 2)
    finish(last)
    attend(groups - 1)

    @pl.loop(0, chunks)
    def _(ch):
        for kind in range(8):
            outgoing(ch, kind).wait_send()

    @pl.loop(0, steps)
    def _(t):
        hop, p = t // PARTS, t % PARTS

        @pl.when((z < depth_z - 1) & (z - hop >= 0))
        def _():
            token_copy(0, hop, p, z - hop).wait_send()

        @pl.when((z > 0) & (z + hop < depth_z))
        def _():
            token_copy(1, hop, p, z + hop).wait_send()

    for copy in (to_sib, to_x, x_to_sib, to_y, y_to_sib):
        copy.wait_send()
    for g in range(groups):
        slab_copy(g).wait()
    final_copy.wait()


def settle(attended, final, attended_out, final_out, held, held_final, sem_in, sem_out):
    rows = attended.shape[0] // PARTS
    heads = final.shape[0] // PARTS
    comes, goes = [], []
    for p in range(PARTS):
        for k, count, source, here, target in (
            (0, rows, attended, held, attended_out),
            (1, heads, final, held_final, final_out),
        ):
            at = pl.ds(p * count, count)
            comes.append(pltpu.make_async_copy(source.at[at], here.at[at], sem_in.at[k, p]))
            goes.append(pltpu.make_async_copy(here.at[at], target.at[at], sem_out.at[k, p]))
    for copy in comes:
        copy.start()
    for copy, onward in zip(comes, goes):
        copy.wait()
        onward.start()
    for onward in goes:
        onward.wait()


def fused(depth_z, tokens, norm_gain, w_query, w_key, w_value, out_gain, carried):
    rows, shard = tokens.shape
    depth, width = w_query.shape
    features = norm_gain.shape[0]
    heads, size = carried.shape[0], carried.shape[1]
    chunks = 3 * (width // GROUP)
    any_spec = pl.BlockSpec(memory_space=pl.ANY)
    vmem_spec = pl.BlockSpec(memory_space=pltpu.VMEM)
    dma = pltpu.SemaphoreType.DMA
    shapes = (
        jax.ShapeDtypeStruct((rows, width), jnp.bfloat16),
        jax.ShapeDtypeStruct(carried.shape, jnp.float32),
    )
    results = pl.pallas_call(
        functools.partial(kernel, depth_z),
        out_shape=shapes,
        in_specs=[any_spec, vmem_spec, any_spec, any_spec, any_spec, vmem_spec, vmem_spec],
        out_specs=(any_spec, any_spec),
        scratch_shapes=[
            pltpu.VMEM((depth_z, rows, shard), jnp.bfloat16),
            pltpu.VMEM((depth_z, rows, shard), jnp.bfloat16),
            pltpu.VMEM((rows, LANES), jnp.float32),
            pltpu.VMEM((rows, GROUP), jnp.float32),
            pltpu.VMEM((chunks, features, GROUP), jnp.bfloat16),
            pltpu.VMEM((chunks, rows, GROUP), jnp.float32),
            pltpu.VMEM((chunks, rows, GROUP), jnp.bfloat16),
            pltpu.VMEM((heads, size, size), jnp.bfloat16),
            pltpu.VMEM((heads, size, size), jnp.bfloat16),
            pltpu.VMEM((2, heads // 2, size, size), jnp.bfloat16),
            pltpu.VMEM((2, heads, size, size), jnp.bfloat16),
            pltpu.VMEM((heads, size, size), jnp.bfloat16),
            dma((chunks + 1,)),
            dma((chunks, 8)),
            dma((chunks, 8)),
            dma((2, depth_z, PARTS)),
            dma((2, depth_z, PARTS)),
            dma((5,)),
            dma((5,)),
            pltpu.VMEM((rows, width), jnp.bfloat16),
            pltpu.VMEM(carried.shape, jnp.float32),
            dma((width // GROUP + 1,)),
        ],
        compiler_params=pltpu.CompilerParams(
            collective_id=0, has_side_effects=True, vmem_limit_bytes=56 * 1024 * 1024
        ),
        cost_estimate=pl.CostEstimate(
            flops=6 * rows * features * width, bytes_accessed=8 * depth * width, transcendentals=0
        ),
    )(tokens, norm_gain.reshape(depth_z, 1, shard), w_query, w_key, w_value, out_gain[None], carried)
    return pl.pallas_call(
        settle,
        out_shape=shapes,
        in_specs=[any_spec, any_spec],
        out_specs=(any_spec, any_spec),
        scratch_shapes=[
            pltpu.VMEM((rows, width), jnp.bfloat16),
            pltpu.VMEM(carried.shape, jnp.float32),
            dma((2, PARTS)),
            dma((2, PARTS)),
        ],
        compiler_params=pltpu.CompilerParams(vmem_limit_bytes=60 * 1024 * 1024),
    )(*results)


def solution(mesh):
    square = mesh.shape["seq"] == 8 and mesh.shape["tensor"] == 4

    def local(tokens, *rest):
        if square and tokens.shape[0] == BLOCK:
            return fused(mesh.shape["tensor"], tokens, *rest)
        return shards(tokens, *rest)

    return jax.shard_map(
        local,
        mesh=mesh,
        in_specs=(
            P("seq", "tensor"),
            P(),
            P("seq", "tensor"),
            P("seq", "tensor"),
            P("seq", "tensor"),
            P("tensor"),
            P("tensor", None, None),
        ),
        out_specs=(P("seq", "tensor"), P("tensor", None, None)),
        check_vma=False,
    )
```

```python
import functools

import jax
import jax.numpy as jnp
from jax import lax
from jax.experimental import pallas as pl
from jax.experimental.pallas import tpu as pltpu
from jax.sharding import PartitionSpec as P

BLOCK = 512
MESH = pl.DeviceIdType.MESH
GROUP = 256
PARTS = 4
AHEAD = 2
LAG = 1
LANES = 128


def add_rows(normed, pieces):
    return tuple((jnp.dot(normed, piece, preferred_element_type=jnp.float32) for piece in pieces))


def shards(tokens, norm_gain, w_query, w_key, w_value, out_gain, carried):
    whole = lax.all_gather(tokens, "tensor", axis=1, tiled=True)
    xf = whole.astype(jnp.float32)
    normed = (xf * lax.rsqrt(jnp.mean(xf * xf, axis=1, keepdims=True) + 1e-05) * norm_gain).astype(
        jnp.bfloat16
    )
    rows = normed.shape[0]
    width = w_query.shape[1]
    size = carried.shape[1]
    heads = width // size
    qsum, ksum, vsum = add_rows(
        normed,
        (
            lax.all_gather(w_query, "seq", axis=0, tiled=True),
            lax.all_gather(w_key, "seq", axis=0, tiled=True),
            lax.all_gather(w_value, "seq", axis=0, tiled=True),
        ),
    )
    blocks = rows // BLOCK
    query = qsum.astype(jnp.bfloat16).reshape(blocks, BLOCK, heads, size)
    key = ksum.astype(jnp.bfloat16).reshape(blocks, BLOCK, heads, size)
    value = vsum.astype(jnp.bfloat16).reshape(blocks, BLOCK, heads, size)
    block_state = jnp.einsum("nthd,nthe->nhde", key, value, preferred_element_type=jnp.float32)
    local_total = jnp.sum(block_state, axis=0)
    zero_state = jnp.zeros_like(local_total)
    mine = lax.axis_index("seq")
    piece = lax.all_gather(
        local_total[None].astype(jnp.bfloat16), "seq", axis=0, tiled=True
    ).astype(jnp.float32)
    where = jnp.arange(piece.shape[0], dtype=jnp.int32)
    keep = (where < mine).astype(jnp.float32)
    before = zero_state + jnp.sum(keep[:, None, None, None] * piece, axis=0)
    total = zero_state + jnp.sum(piece, axis=0)
    start_state = carried + before
    running = jnp.cumsum(block_state, axis=0) - block_state
    priors = start_state[None] + running
    inter = jnp.einsum(
        "nthd,nhde->nthe", query.astype(jnp.float32), priors, precision=lax.Precision.HIGHEST
    )
    causal = jnp.tril(jnp.ones((BLOCK, BLOCK), jnp.float32))
    scores = jnp.einsum("nthd,nshd->nhts", query, key, preferred_element_type=jnp.float32)
    weights = (scores * causal).astype(jnp.bfloat16)
    intra = jnp.einsum("nhts,nshe->nthe", weights, value, preferred_element_type=jnp.float32)
    raw = inter + intra
    normal = (
        raw
        * lax.rsqrt(jnp.mean(raw * raw, axis=3, keepdims=True) + 1e-06)
        * out_gain.reshape(heads, size)
    )
    attended = normal.astype(jnp.bfloat16).reshape(rows, width)
    return (attended, carried + total)


def dot(a, b, dims=((1,), (0,))):
    return lax.dot_general(a, b, (dims, ((), ())), preferred_element_type=jnp.float32)


def kernel(
    depth_z,
    tokens,
    norm_gain,
    w_query,
    w_key,
    w_value,
    out_gain,
    carried,
    attended,
    final,
    tok,
    scaled,
    squares,
    row_scale,
    buf,
    acc,
    proj,
    state_out,
    state_sib,
    sum_out,
    sum_in,
    prior,
    local_sem,
    w_send,
    w_recv,
    t_send,
    t_recv,
    s_send,
    s_recv,
):
    rows, shard = tokens.shape
    depth = w_query.shape[0]
    groups = w_query.shape[1] // GROUP
    size = carried.shape[1]
    heads = carried.shape[0]
    per = GROUP // size
    half = heads // 2
    early = 2 * groups
    chunks = 3 * groups
    part = rows // PARTS
    hops = depth_z - 1

    seq = lax.axis_index("seq")
    z = lax.axis_index("tensor")
    c = seq % 2
    x = (seq // 2) % 2
    y = seq // 4
    sib = y * 4 + x * 2 + (1 - c)
    xn = y * 4 + (1 - x) * 2 + c
    yn = (1 - y) * 4 + x * 2 + c
    diag = (1 - y) * 4 + (1 - x) * 2 + c
    x_sib = y * 4 + (1 - x) * 2 + (1 - c)
    y_sib = (1 - y) * 4 + x * 2 + (1 - c)
    diag_sib = (1 - y) * 4 + (1 - x) * 2 + (1 - c)

    tok_copy = pltpu.make_async_copy(tokens, tok.at[z], local_sem.at[chunks])
    tok_copy.start()
    own_copies = []
    for ch in range(chunks):
        if ch < early:
            ref, g = (w_key, w_value)[ch % 2], ch // 2
        else:
            ref, g = w_query, ch - early
        copy = pltpu.make_async_copy(
            ref.at[:, pl.ds(g * GROUP, GROUP)],
            buf.at[ch, pl.ds(pl.multiple_of(seq * depth, depth), depth), :],
            local_sem.at[ch],
        )
        copy.start()
        own_copies.append(copy)

    barrier = pltpu.get_barrier_semaphore()
    for other in (sib, xn, yn):
        pl.semaphore_signal(barrier, inc=1, device_id=(other, z), device_id_type=MESH)

    @pl.when(z > 0)
    def _():
        pl.semaphore_signal(barrier, inc=1, device_id=(seq, z - 1), device_id_type=MESH)

    @pl.when(z < depth_z - 1)
    def _():
        pl.semaphore_signal(barrier, inc=1, device_id=(seq, z + 1), device_id_type=MESH)

    pl.semaphore_wait(barrier, 3 + jnp.minimum(z, 1) + jnp.minimum(depth_z - 1 - z, 1))

    def piece(ch, kind, owner, target, first=0, count=None):
        count = depth if count is None else count
        at = buf.at[ch, pl.ds(pl.multiple_of(owner * depth + first, count), count), :]
        return pltpu.make_async_remote_copy(
            src_ref=at,
            dst_ref=at,
            send_sem=w_send.at[ch, kind],
            recv_sem=w_recv.at[ch, kind],
            device_id=(target, z),
            device_id_type=MESH,
        )

    mid = depth // 2

    def outgoing(ch, kind):
        places = (
            (seq, xn),
            (seq, yn),
            (seq, sib),
            (xn, yn, 0, mid),
            (yn, xn, mid, mid),
            (xn, sib),
            (yn, sib),
            (diag, sib),
        )
        return piece(ch, kind, *places[kind])

    def incoming(ch, kind):
        places = (
            (xn, xn),
            (yn, yn),
            (sib, sib),
            (diag, yn, 0, mid),
            (diag, xn, mid, mid),
            (x_sib, sib),
            (y_sib, sib),
            (diag_sib, sib),
        )
        return piece(ch, kind, *places[kind])

    def send_own(ch):
        for kind in (0, 1, 2):
            outgoing(ch, kind).start()

    def pass_near(ch):
        incoming(ch, 0).wait_recv()
        outgoing(ch, 3).start()
        outgoing(ch, 5).start()
        incoming(ch, 1).wait_recv()
        outgoing(ch, 4).start()
        outgoing(ch, 6).start()

    def pass_far(ch):
        incoming(ch, 3).wait_recv()
        incoming(ch, 4).wait_recv()
        outgoing(ch, 7).start()

    def complete(ch):
        for kind in (2, 5, 6, 7):
            incoming(ch, kind).wait_recv()

    def token_copy(way, hop, p, owner):
        at = tok.at[owner, pl.ds(pl.multiple_of(p * part, part), part), :]
        target = z + 1 if way == 0 else z - 1
        return pltpu.make_async_remote_copy(
            src_ref=at,
            dst_ref=at,
            send_sem=t_send.at[way, hop, p],
            recv_sem=t_recv.at[way, hop, p],
            device_id=(seq, target),
            device_id_type=MESH,
        )

    def token_step(t):
        hop, p = t // PARTS, t % PARTS

        @pl.when(z - 1 - hop >= 0)
        def _():
            token_copy(0, hop, p, z - 1 - hop).wait_recv()

            @pl.when(z < depth_z - 1)
            def _():
                token_copy(0, hop + 1, p, z - 1 - hop).start()

        @pl.when(z + 1 + hop < depth_z)
        def _():
            token_copy(1, hop, p, z + 1 + hop).wait_recv()

            @pl.when(z > 0)
            def _():
                token_copy(1, hop + 1, p, z + 1 + hop).start()

    own_copies[0].wait()
    send_own(0)
    tok_copy.wait()

    @pl.loop(0, PARTS)
    def _(p):
        @pl.when(z < depth_z - 1)
        def _():
            token_copy(0, 0, p, z).start()

        @pl.when(z > 0)
        def _():
            token_copy(1, 0, p, z).start()

    for ch in range(1, chunks):
        own_copies[ch].wait()
    for ch in range(1, AHEAD):
        send_own(ch)

    def convert(k):
        step = 32

        @pl.loop(0, rows // step)
        def _(r):
            at = pl.ds(pl.multiple_of(r * step, step), step)
            v = tok[k, at, :].astype(jnp.float32)
            scaled[k, at, :] = (v * norm_gain[k]).astype(jnp.bfloat16)
            v = v * v
            total = squares[at, :]
            for f in range(shard // LANES):
                total = total + v[:, f * LANES : (f + 1) * LANES]
            squares[at, :] = total

    def find_scale():
        mean = jnp.sum(squares[...], axis=1, keepdims=True) / (depth_z * shard)
        row_scale[...] = jnp.broadcast_to(lax.rsqrt(mean + 1e-05), (rows, GROUP))

    def accumulate(ch, k):
        at = pl.ds(pl.multiple_of(k * shard, shard), shard)
        acc[ch] += dot(scaled[k], buf[ch, at, :])

    def finish(ch):
        proj[ch] = (acc[ch] * row_scale[...]).astype(jnp.bfloat16)

        @pl.when((ch % 2 == 1) & (ch < early))
        def _():
            both = dot(proj[ch - 1], proj[ch], ((0,), (0,)))
            for e in range(per):
                st = both[e * size : (e + 1) * size, e * size : (e + 1) * size]
                state_out[ch // 2 * per + e] = st.astype(jnp.bfloat16)

    def begin(ch, first, last):
        complete(ch)
        acc[ch] = jnp.zeros((rows, GROUP), jnp.float32)

        @pl.loop(first, last)
        def _(k):
            accumulate(ch, k)

    def project(ch):
        begin(ch, 0, depth_z)
        finish(ch)

    mine = pl.ds(c * half, half)
    theirs = pl.ds((1 - c) * half, half)

    def state_copy(k, source, target_ref, target):
        return pltpu.make_async_remote_copy(
            src_ref=source,
            dst_ref=target_ref,
            send_sem=s_send.at[k],
            recv_sem=s_recv.at[k],
            device_id=(target, z),
            device_id_type=MESH,
        )

    to_sib = state_copy(0, state_out, state_sib, sib)
    to_x = state_copy(1, sum_out.at[0], sum_in.at[0, mine], xn)
    x_to_sib = state_copy(2, sum_in.at[0, mine], sum_in.at[0, mine], sib)
    to_y = state_copy(3, sum_out.at[1], sum_in.at[1, mine], yn)
    y_to_sib = state_copy(4, sum_in.at[1, mine], sum_in.at[1, mine], sib)
    x_from_sib = state_copy(2, sum_in.at[0, theirs], sum_in.at[0, theirs], sib)
    y_from_sib = state_copy(4, sum_in.at[1, theirs], sum_in.at[1, theirs], sib)

    def wide(v):
        return v.astype(jnp.float32)

    def state_one():
        to_sib.start()

    def state_two():
        to_sib.wait_recv()
        sum_out[0] = (wide(state_out[mine]) + wide(state_sib[mine])).astype(jnp.bfloat16)
        to_x.start()

    def state_three():
        to_x.wait_recv()
        x_to_sib.start()
        sum_out[1] = (wide(sum_out[0]) + wide(sum_in[0, mine])).astype(jnp.bfloat16)
        to_y.start()

    def state_four():
        to_y.wait_recv()
        y_to_sib.start()

    def state_five():
        x_from_sib.wait_recv()
        y_from_sib.wait_recv()
        on_c = c.astype(jnp.float32)
        on_x = x.astype(jnp.float32)
        on_y = y.astype(jnp.float32)
        for h in range(heads):
            near = wide(state_sib[h])
            chip = (wide(state_out[h]) + near).astype(jnp.bfloat16)
            beside = wide(sum_in[0, h])
            row = (wide(chip) + beside).astype(jnp.bfloat16)
            far = wide(sum_in[1, h])
            start = carried[h]
            before = near * on_c + beside * on_x + far * on_y
            prior[h] = (start + before).astype(jnp.bfloat16)
            final[h] = start + (wide(row) + far)

    top = rows // 2

    def attend(g):
        at = lax.broadcasted_iota(jnp.int32, (top, top), 0)
        of = lax.broadcasted_iota(jnp.int32, (top, top), 1)
        causal = of <= at

        def masked(s):
            return jnp.where(causal, s, 0.0).astype(jnp.bfloat16)

        for e in range(per):
            cols = slice(e * size, (e + 1) * size)
            h = g * per + e
            start = prior[h]
            q0, q1 = proj[early + g, :top, cols], proj[early + g, top:, cols]
            k0, k1 = proj[2 * g, :top, cols], proj[2 * g, top:, cols]
            v0, v1 = proj[2 * g + 1, :top, cols], proj[2 * g + 1, top:, cols]
            across = ((1,), (1,))
            raw0 = dot(q0, start) + dot(masked(dot(q0, k0, across)), v0)
            raw1 = (
                dot(q1, start)
                + dot(dot(q1, k0, across).astype(jnp.bfloat16), v0)
                + dot(masked(dot(q1, k1, across)), v1)
            )
            gain = out_gain[:, h * size : (h + 1) * size]
            for first, raw in ((0, raw0), (top, raw1)):
                scale = lax.rsqrt(jnp.mean(raw * raw, axis=1, keepdims=True) + 1e-06)
                attended[first : first + top, h * size : (h + 1) * size] = (
                    raw * scale * gain
                ).astype(jnp.bfloat16)

    steps = hops * PARTS

    squares[...] = jnp.zeros_like(squares)
    convert(z)

    @pl.loop(0, early)
    def _(i):
        pass_near(i)
        send_own(i + AHEAD)

        @pl.when(i >= LAG)
        def _():
            pass_far(i - LAG)

        first = jnp.minimum(i * steps // early, steps)
        last = jnp.minimum((i + 1) * steps // early, steps)

        @pl.loop(first, last)
        def _(t):
            token_step(t)

        level = last // PARTS
        now = i - LAG - 1

        @pl.when(level > first // PARTS)
        def _():
            for k in (z - level, z + level):

                @pl.when((k >= 0) & (k < depth_z))
                def _(k=k):
                    convert(k)

                    @pl.loop(0, now)
                    def _(ch):
                        accumulate(ch, k)

            @pl.when(level == hops)
            def _():
                find_scale()

                @pl.loop(0, now)
                def _(ch):
                    finish(ch)

        @pl.when(now >= 0)
        def _():
            begin(now, jnp.maximum(z - level, 0), jnp.minimum(z + level + 1, depth_z))

            @pl.when(level == hops)
            def _():
                finish(now)

    pass_near(early)
    pass_far(early - 1)

    @pl.loop(early - LAG - 1, early)
    def _(ch):
        project(ch)

    state_one()
    state_two()
    send_own(early + 2)
    for g in range(1, groups - 1):
        i = early + g
        pass_near(i)
        pass_far(i - 1)
        if g == 1:
            state_three()
        if g == groups - 2:
            state_four()
        if i + AHEAD < chunks:
            send_own(i + AHEAD)
        project(i - 1)
    state_five()
    for g in range(groups - 2):
        attend(g)

    last = chunks - 1
    pass_near(last)
    acc[last] = jnp.zeros((rows, GROUP), jnp.float32)
    for kind, owner in ((2, seq), (5, xn), (6, yn)):
        incoming(last, kind).wait_recv()
        accumulate(last, owner // 2)
    pass_far(last - 1)
    project(last - 1)
    pass_far(last)
    attend(groups - 2)
    incoming(last, 7).wait_recv()
    accumulate(last, diag // 2)
    finish(last)
    attend(groups - 1)

    @pl.loop(0, chunks)
    def _(ch):
        for kind in range(8):
            outgoing(ch, kind).wait_send()

    @pl.loop(0, steps)
    def _(t):
        hop, p = t // PARTS, t % PARTS

        @pl.when((z < depth_z - 1) & (z - hop >= 0))
        def _():
            token_copy(0, hop, p, z - hop).wait_send()

        @pl.when((z > 0) & (z + hop < depth_z))
        def _():
            token_copy(1, hop, p, z + hop).wait_send()

    for copy in (to_sib, to_x, x_to_sib, to_y, y_to_sib):
        copy.wait_send()


def settle(attended, final, attended_out, final_out, sems):
    rows = attended.shape[0] // PARTS
    heads = final.shape[0] // PARTS
    copies = []
    for p in range(PARTS):
        at = pl.ds(p * rows, rows)
        copies.append(pltpu.make_async_copy(attended.at[at], attended_out.at[at], sems.at[0, p]))
        at = pl.ds(p * heads, heads)
        copies.append(pltpu.make_async_copy(final.at[at], final_out.at[at], sems.at[1, p]))
    for copy in copies:
        copy.start()
    for copy in copies:
        copy.wait()


def fused(depth_z, tokens, norm_gain, w_query, w_key, w_value, out_gain, carried):
    rows, shard = tokens.shape
    depth, width = w_query.shape
    features = norm_gain.shape[0]
    heads, size = carried.shape[0], carried.shape[1]
    chunks = 3 * (width // GROUP)
    any_spec = pl.BlockSpec(memory_space=pl.ANY)
    vmem_spec = pl.BlockSpec(memory_space=pltpu.VMEM)
    dma = pltpu.SemaphoreType.DMA
    shapes = (
        jax.ShapeDtypeStruct((rows, width), jnp.bfloat16),
        jax.ShapeDtypeStruct(carried.shape, jnp.float32),
    )
    results = pl.pallas_call(
        functools.partial(kernel, depth_z),
        out_shape=tuple(pltpu.VMEM(s.shape, s.dtype) for s in shapes),
        in_specs=[any_spec, vmem_spec, any_spec, any_spec, any_spec, vmem_spec, vmem_spec],
        out_specs=(vmem_spec, vmem_spec),
        scratch_shapes=[
            pltpu.VMEM((depth_z, rows, shard), jnp.bfloat16),
            pltpu.VMEM((depth_z, rows, shard), jnp.bfloat16),
            pltpu.VMEM((rows, LANES), jnp.float32),
            pltpu.VMEM((rows, GROUP), jnp.float32),
            pltpu.VMEM((chunks, features, GROUP), jnp.bfloat16),
            pltpu.VMEM((chunks, rows, GROUP), jnp.float32),
            pltpu.VMEM((chunks, rows, GROUP), jnp.bfloat16),
            pltpu.VMEM((heads, size, size), jnp.bfloat16),
            pltpu.VMEM((heads, size, size), jnp.bfloat16),
            pltpu.VMEM((2, heads // 2, size, size), jnp.bfloat16),
            pltpu.VMEM((2, heads, size, size), jnp.bfloat16),
            pltpu.VMEM((heads, size, size), jnp.bfloat16),
            dma((chunks + 1,)),
            dma((chunks, 8)),
            dma((chunks, 8)),
            dma((2, depth_z, PARTS)),
            dma((2, depth_z, PARTS)),
            dma((5,)),
            dma((5,)),
        ],
        compiler_params=pltpu.CompilerParams(
            collective_id=0, has_side_effects=True, vmem_limit_bytes=56 * 1024 * 1024
        ),
        cost_estimate=pl.CostEstimate(
            flops=6 * rows * features * width, bytes_accessed=8 * depth * width, transcendentals=0
        ),
    )(tokens, norm_gain.reshape(depth_z, 1, shard), w_query, w_key, w_value, out_gain[None], carried)
    return pl.pallas_call(
        settle,
        out_shape=shapes,
        in_specs=[any_spec, any_spec],
        out_specs=(any_spec, any_spec),
        scratch_shapes=[dma((2, PARTS))],
    )(*results)


def solution(mesh):
    square = mesh.shape["seq"] == 8 and mesh.shape["tensor"] == 4

    def local(tokens, *rest):
        if square and tokens.shape[0] == BLOCK:
            return fused(mesh.shape["tensor"], tokens, *rest)
        return shards(tokens, *rest)

    return jax.shard_map(
        local,
        mesh=mesh,
        in_specs=(
            P("seq", "tensor"),
            P(),
            P("seq", "tensor"),
            P("seq", "tensor"),
            P("seq", "tensor"),
            P("tensor"),
            P("tensor", None, None),
        ),
        out_specs=(P("seq", "tensor"), P("tensor", None, None)),
        check_vma=False,
    )
```

```python
import functools

import jax
import jax.numpy as jnp
from jax import lax
from jax.experimental import pallas as pl
from jax.experimental.pallas import tpu as pltpu
from jax.sharding import PartitionSpec as P

BLOCK = 512
MESH = pl.DeviceIdType.MESH
GROUP = 256
PARTS = 4
AHEAD = 2
LAG = 1
LANES = 128


def add_rows(normed, pieces):
    return tuple((jnp.dot(normed, piece, preferred_element_type=jnp.float32) for piece in pieces))


def shards(tokens, norm_gain, w_query, w_key, w_value, out_gain, carried):
    whole = lax.all_gather(tokens, "tensor", axis=1, tiled=True)
    xf = whole.astype(jnp.float32)
    normed = (xf * lax.rsqrt(jnp.mean(xf * xf, axis=1, keepdims=True) + 1e-05) * norm_gain).astype(
        jnp.bfloat16
    )
    rows = normed.shape[0]
    width = w_query.shape[1]
    size = carried.shape[1]
    heads = width // size
    qsum, ksum, vsum = add_rows(
        normed,
        (
            lax.all_gather(w_query, "seq", axis=0, tiled=True),
            lax.all_gather(w_key, "seq", axis=0, tiled=True),
            lax.all_gather(w_value, "seq", axis=0, tiled=True),
        ),
    )
    blocks = rows // BLOCK
    query = qsum.astype(jnp.bfloat16).reshape(blocks, BLOCK, heads, size)
    key = ksum.astype(jnp.bfloat16).reshape(blocks, BLOCK, heads, size)
    value = vsum.astype(jnp.bfloat16).reshape(blocks, BLOCK, heads, size)
    block_state = jnp.einsum("nthd,nthe->nhde", key, value, preferred_element_type=jnp.float32)
    local_total = jnp.sum(block_state, axis=0)
    zero_state = jnp.zeros_like(local_total)
    mine = lax.axis_index("seq")
    piece = lax.all_gather(
        local_total[None].astype(jnp.bfloat16), "seq", axis=0, tiled=True
    ).astype(jnp.float32)
    where = jnp.arange(piece.shape[0], dtype=jnp.int32)
    keep = (where < mine).astype(jnp.float32)
    before = zero_state + jnp.sum(keep[:, None, None, None] * piece, axis=0)
    total = zero_state + jnp.sum(piece, axis=0)
    start_state = carried + before
    running = jnp.cumsum(block_state, axis=0) - block_state
    priors = start_state[None] + running
    inter = jnp.einsum(
        "nthd,nhde->nthe", query.astype(jnp.float32), priors, precision=lax.Precision.HIGHEST
    )
    causal = jnp.tril(jnp.ones((BLOCK, BLOCK), jnp.float32))
    scores = jnp.einsum("nthd,nshd->nhts", query, key, preferred_element_type=jnp.float32)
    weights = (scores * causal).astype(jnp.bfloat16)
    intra = jnp.einsum("nhts,nshe->nthe", weights, value, preferred_element_type=jnp.float32)
    raw = inter + intra
    normal = (
        raw
        * lax.rsqrt(jnp.mean(raw * raw, axis=3, keepdims=True) + 1e-06)
        * out_gain.reshape(heads, size)
    )
    attended = normal.astype(jnp.bfloat16).reshape(rows, width)
    return (attended, carried + total)


def dot(a, b, dims=((1,), (0,))):
    return lax.dot_general(a, b, (dims, ((), ())), preferred_element_type=jnp.float32)


def kernel(
    depth_z,
    tokens,
    norm_gain,
    w_query,
    w_key,
    w_value,
    out_gain,
    carried,
    attended,
    final,
    tok,
    scaled,
    squares,
    row_scale,
    buf,
    acc,
    proj,
    state_out,
    state_sib,
    sum_out,
    sum_in,
    prior,
    local_sem,
    w_send,
    w_recv,
    t_send,
    t_recv,
    s_send,
    s_recv,
):
    rows, shard = tokens.shape
    depth = w_query.shape[0]
    groups = w_query.shape[1] // GROUP
    size = carried.shape[1]
    heads = carried.shape[0]
    per = GROUP // size
    half = heads // 2
    early = 2 * groups
    chunks = 3 * groups
    part = rows // PARTS
    hops = depth_z - 1

    seq = lax.axis_index("seq")
    z = lax.axis_index("tensor")
    c = seq % 2
    x = (seq // 2) % 2
    y = seq // 4
    sib = y * 4 + x * 2 + (1 - c)
    xn = y * 4 + (1 - x) * 2 + c
    yn = (1 - y) * 4 + x * 2 + c
    diag = (1 - y) * 4 + (1 - x) * 2 + c
    x_sib = y * 4 + (1 - x) * 2 + (1 - c)
    y_sib = (1 - y) * 4 + x * 2 + (1 - c)
    diag_sib = (1 - y) * 4 + (1 - x) * 2 + (1 - c)

    tok_copy = pltpu.make_async_copy(tokens, tok.at[z], local_sem.at[chunks])
    tok_copy.start()
    own_copies = []
    for ch in range(chunks):
        if ch < early:
            ref, g = (w_key, w_value)[ch % 2], ch // 2
        else:
            ref, g = w_query, ch - early
        copy = pltpu.make_async_copy(
            ref.at[:, pl.ds(g * GROUP, GROUP)],
            buf.at[ch, pl.ds(pl.multiple_of(seq * depth, depth), depth), :],
            local_sem.at[ch],
        )
        copy.start()
        own_copies.append(copy)

    barrier = pltpu.get_barrier_semaphore()
    for other in (sib, xn, yn):
        pl.semaphore_signal(barrier, inc=1, device_id=(other, z), device_id_type=MESH)

    @pl.when(z > 0)
    def _():
        pl.semaphore_signal(barrier, inc=1, device_id=(seq, z - 1), device_id_type=MESH)

    @pl.when(z < depth_z - 1)
    def _():
        pl.semaphore_signal(barrier, inc=1, device_id=(seq, z + 1), device_id_type=MESH)

    pl.semaphore_wait(barrier, 3 + jnp.minimum(z, 1) + jnp.minimum(depth_z - 1 - z, 1))

    def piece(ch, kind, owner, target, first=0, count=None):
        count = depth if count is None else count
        at = buf.at[ch, pl.ds(pl.multiple_of(owner * depth + first, count), count), :]
        return pltpu.make_async_remote_copy(
            src_ref=at,
            dst_ref=at,
            send_sem=w_send.at[ch, kind],
            recv_sem=w_recv.at[ch, kind],
            device_id=(target, z),
            device_id_type=MESH,
        )

    mid = depth // 2

    def outgoing(ch, kind):
        places = (
            (seq, xn),
            (seq, yn),
            (seq, sib),
            (xn, yn, 0, mid),
            (yn, xn, mid, mid),
            (xn, sib),
            (yn, sib),
            (diag, sib),
        )
        return piece(ch, kind, *places[kind])

    def incoming(ch, kind):
        places = (
            (xn, xn),
            (yn, yn),
            (sib, sib),
            (diag, yn, 0, mid),
            (diag, xn, mid, mid),
            (x_sib, sib),
            (y_sib, sib),
            (diag_sib, sib),
        )
        return piece(ch, kind, *places[kind])

    def send_own(ch):
        for kind in (0, 1, 2):
            outgoing(ch, kind).start()

    def pass_near(ch):
        incoming(ch, 0).wait_recv()
        outgoing(ch, 3).start()
        outgoing(ch, 5).start()
        incoming(ch, 1).wait_recv()
        outgoing(ch, 4).start()
        outgoing(ch, 6).start()

    def pass_far(ch):
        incoming(ch, 3).wait_recv()
        incoming(ch, 4).wait_recv()
        outgoing(ch, 7).start()

    def complete(ch):
        for kind in (2, 5, 6, 7):
            incoming(ch, kind).wait_recv()

    def token_copy(way, hop, p, owner):
        at = tok.at[owner, pl.ds(pl.multiple_of(p * part, part), part), :]
        target = z + 1 if way == 0 else z - 1
        return pltpu.make_async_remote_copy(
            src_ref=at,
            dst_ref=at,
            send_sem=t_send.at[way, hop, p],
            recv_sem=t_recv.at[way, hop, p],
            device_id=(seq, target),
            device_id_type=MESH,
        )

    def token_step(t):
        hop, p = t // PARTS, t % PARTS

        @pl.when(z - 1 - hop >= 0)
        def _():
            token_copy(0, hop, p, z - 1 - hop).wait_recv()

            @pl.when(z < depth_z - 1)
            def _():
                token_copy(0, hop + 1, p, z - 1 - hop).start()

        @pl.when(z + 1 + hop < depth_z)
        def _():
            token_copy(1, hop, p, z + 1 + hop).wait_recv()

            @pl.when(z > 0)
            def _():
                token_copy(1, hop + 1, p, z + 1 + hop).start()

    own_copies[0].wait()
    send_own(0)
    tok_copy.wait()

    @pl.loop(0, PARTS)
    def _(p):
        @pl.when(z < depth_z - 1)
        def _():
            token_copy(0, 0, p, z).start()

        @pl.when(z > 0)
        def _():
            token_copy(1, 0, p, z).start()

    for ch in range(1, chunks):
        own_copies[ch].wait()
    for ch in range(1, AHEAD):
        send_own(ch)

    def convert(k):
        step = 32

        @pl.loop(0, rows // step)
        def _(r):
            at = pl.ds(pl.multiple_of(r * step, step), step)
            v = tok[k, at, :].astype(jnp.float32)
            scaled[k, at, :] = (v * norm_gain[k]).astype(jnp.bfloat16)
            v = v * v
            total = squares[at, :]
            for f in range(shard // LANES):
                total = total + v[:, f * LANES : (f + 1) * LANES]
            squares[at, :] = total

    def find_scale():
        mean = jnp.sum(squares[...], axis=1, keepdims=True) / (depth_z * shard)
        row_scale[...] = jnp.broadcast_to(lax.rsqrt(mean + 1e-05), (rows, GROUP))

    def accumulate(ch, k):
        at = pl.ds(pl.multiple_of(k * shard, shard), shard)
        acc[ch] += dot(scaled[k], buf[ch, at, :])

    def finish(ch):
        proj[ch] = (acc[ch] * row_scale[...]).astype(jnp.bfloat16)

        @pl.when((ch % 2 == 1) & (ch < early))
        def _():
            both = dot(proj[ch - 1], proj[ch], ((0,), (0,)))
            for e in range(per):
                st = both[e * size : (e + 1) * size, e * size : (e + 1) * size]
                state_out[ch // 2 * per + e] = st.astype(jnp.bfloat16)

    def begin(ch, first, last):
        complete(ch)
        acc[ch] = jnp.zeros((rows, GROUP), jnp.float32)

        @pl.loop(first, last)
        def _(k):
            accumulate(ch, k)

    def project(ch):
        begin(ch, 0, depth_z)
        finish(ch)

    mine = pl.ds(c * half, half)
    theirs = pl.ds((1 - c) * half, half)

    def state_copy(k, source, target_ref, target):
        return pltpu.make_async_remote_copy(
            src_ref=source,
            dst_ref=target_ref,
            send_sem=s_send.at[k],
            recv_sem=s_recv.at[k],
            device_id=(target, z),
            device_id_type=MESH,
        )

    to_sib = state_copy(0, state_out, state_sib, sib)
    to_x = state_copy(1, sum_out.at[0], sum_in.at[0, mine], xn)
    x_to_sib = state_copy(2, sum_in.at[0, mine], sum_in.at[0, mine], sib)
    to_y = state_copy(3, sum_out.at[1], sum_in.at[1, mine], yn)
    y_to_sib = state_copy(4, sum_in.at[1, mine], sum_in.at[1, mine], sib)
    x_from_sib = state_copy(2, sum_in.at[0, theirs], sum_in.at[0, theirs], sib)
    y_from_sib = state_copy(4, sum_in.at[1, theirs], sum_in.at[1, theirs], sib)

    def wide(v):
        return v.astype(jnp.float32)

    def state_one():
        to_sib.start()

    def state_two():
        to_sib.wait_recv()
        sum_out[0] = (wide(state_out[mine]) + wide(state_sib[mine])).astype(jnp.bfloat16)
        to_x.start()

    def state_three():
        to_x.wait_recv()
        x_to_sib.start()
        sum_out[1] = (wide(sum_out[0]) + wide(sum_in[0, mine])).astype(jnp.bfloat16)
        to_y.start()

    def state_four():
        to_y.wait_recv()
        y_to_sib.start()

    def state_five():
        x_from_sib.wait_recv()
        y_from_sib.wait_recv()
        on_c = c.astype(jnp.float32)
        on_x = x.astype(jnp.float32)
        on_y = y.astype(jnp.float32)
        for h in range(heads):
            near = wide(state_sib[h])
            chip = (wide(state_out[h]) + near).astype(jnp.bfloat16)
            beside = wide(sum_in[0, h])
            row = (wide(chip) + beside).astype(jnp.bfloat16)
            far = wide(sum_in[1, h])
            start = carried[h]
            before = near * on_c + beside * on_x + far * on_y
            prior[h] = (start + before).astype(jnp.bfloat16)
            final[h] = start + (wide(row) + far)

    top = rows // 2

    def attend(g):
        at = lax.broadcasted_iota(jnp.int32, (top, top), 0)
        of = lax.broadcasted_iota(jnp.int32, (top, top), 1)
        causal = of <= at

        def masked(s):
            return jnp.where(causal, s, 0.0).astype(jnp.bfloat16)

        for e in range(per):
            cols = slice(e * size, (e + 1) * size)
            h = g * per + e
            start = prior[h]
            q0, q1 = proj[early + g, :top, cols], proj[early + g, top:, cols]
            k0, k1 = proj[2 * g, :top, cols], proj[2 * g, top:, cols]
            v0, v1 = proj[2 * g + 1, :top, cols], proj[2 * g + 1, top:, cols]
            across = ((1,), (1,))
            raw0 = dot(q0, start) + dot(masked(dot(q0, k0, across)), v0)
            raw1 = (
                dot(q1, start)
                + dot(dot(q1, k0, across).astype(jnp.bfloat16), v0)
                + dot(masked(dot(q1, k1, across)), v1)
            )
            gain = out_gain[:, h * size : (h + 1) * size]
            for first, raw in ((0, raw0), (top, raw1)):
                scale = lax.rsqrt(jnp.mean(raw * raw, axis=1, keepdims=True) + 1e-06)
                attended[first : first + top, h * size : (h + 1) * size] = (
                    raw * scale * gain
                ).astype(jnp.bfloat16)

    steps = hops * PARTS

    squares[...] = jnp.zeros_like(squares)
    convert(z)

    @pl.loop(0, early)
    def _(i):
        pass_near(i)
        send_own(i + AHEAD)

        @pl.when(i >= LAG)
        def _():
            pass_far(i - LAG)

        first = jnp.minimum(i * steps // early, steps)
        last = jnp.minimum((i + 1) * steps // early, steps)

        @pl.loop(first, last)
        def _(t):
            token_step(t)

        level = last // PARTS
        now = i - LAG - 1

        @pl.when(level > first // PARTS)
        def _():
            for k in (z - level, z + level):

                @pl.when((k >= 0) & (k < depth_z))
                def _(k=k):
                    convert(k)

                    @pl.loop(0, now)
                    def _(ch):
                        accumulate(ch, k)

            @pl.when(level == hops)
            def _():
                find_scale()

                @pl.loop(0, now)
                def _(ch):
                    finish(ch)

        @pl.when(now >= 0)
        def _():
            begin(now, jnp.maximum(z - level, 0), jnp.minimum(z + level + 1, depth_z))

            @pl.when(level == hops)
            def _():
                finish(now)

    pass_near(early)
    pass_far(early - 1)

    @pl.loop(early - LAG - 1, early)
    def _(ch):
        project(ch)

    state_one()
    state_two()
    send_own(early + 2)
    for g in range(1, groups - 1):
        i = early + g
        pass_near(i)
        pass_far(i - 1)
        if g == 1:
            state_three()
        if g == groups - 2:
            state_four()
        if i + AHEAD < chunks:
            send_own(i + AHEAD)
        project(i - 1)
    state_five()
    for g in range(groups - 2):
        attend(g)

    last = chunks - 1
    pass_near(last)
    acc[last] = jnp.zeros((rows, GROUP), jnp.float32)
    for kind, owner in ((2, seq), (5, xn), (6, yn)):
        incoming(last, kind).wait_recv()
        accumulate(last, owner // 2)
    pass_far(last - 1)
    project(last - 1)
    pass_far(last)
    attend(groups - 2)
    incoming(last, 7).wait_recv()
    accumulate(last, diag // 2)
    finish(last)
    attend(groups - 1)

    @pl.loop(0, chunks)
    def _(ch):
        for kind in range(8):
            outgoing(ch, kind).wait_send()

    @pl.loop(0, steps)
    def _(t):
        hop, p = t // PARTS, t % PARTS

        @pl.when((z < depth_z - 1) & (z - hop >= 0))
        def _():
            token_copy(0, hop, p, z - hop).wait_send()

        @pl.when((z > 0) & (z + hop < depth_z))
        def _():
            token_copy(1, hop, p, z + hop).wait_send()

    for copy in (to_sib, to_x, x_to_sib, to_y, y_to_sib):
        copy.wait_send()


def fused(depth_z, tokens, norm_gain, w_query, w_key, w_value, out_gain, carried):
    rows, shard = tokens.shape
    depth, width = w_query.shape
    features = norm_gain.shape[0]
    heads, size = carried.shape[0], carried.shape[1]
    chunks = 3 * (width // GROUP)
    any_spec = pl.BlockSpec(memory_space=pl.ANY)
    vmem_spec = pl.BlockSpec(memory_space=pltpu.VMEM)
    dma = pltpu.SemaphoreType.DMA
    shapes = (
        jax.ShapeDtypeStruct((rows, width), jnp.bfloat16),
        jax.ShapeDtypeStruct(carried.shape, jnp.float32),
    )
    return pl.pallas_call(
        functools.partial(kernel, depth_z),
        out_shape=tuple(pltpu.VMEM(s.shape, s.dtype) for s in shapes),
        in_specs=[any_spec, vmem_spec, any_spec, any_spec, any_spec, vmem_spec, vmem_spec],
        out_specs=(vmem_spec, vmem_spec),
        scratch_shapes=[
            pltpu.VMEM((depth_z, rows, shard), jnp.bfloat16),
            pltpu.VMEM((depth_z, rows, shard), jnp.bfloat16),
            pltpu.VMEM((rows, LANES), jnp.float32),
            pltpu.VMEM((rows, GROUP), jnp.float32),
            pltpu.VMEM((chunks, features, GROUP), jnp.bfloat16),
            pltpu.VMEM((chunks, rows, GROUP), jnp.float32),
            pltpu.VMEM((chunks, rows, GROUP), jnp.bfloat16),
            pltpu.VMEM((heads, size, size), jnp.bfloat16),
            pltpu.VMEM((heads, size, size), jnp.bfloat16),
            pltpu.VMEM((2, heads // 2, size, size), jnp.bfloat16),
            pltpu.VMEM((2, heads, size, size), jnp.bfloat16),
            pltpu.VMEM((heads, size, size), jnp.bfloat16),
            dma((chunks + 1,)),
            dma((chunks, 8)),
            dma((chunks, 8)),
            dma((2, depth_z, PARTS)),
            dma((2, depth_z, PARTS)),
            dma((5,)),
            dma((5,)),
        ],
        compiler_params=pltpu.CompilerParams(
            collective_id=0, has_side_effects=True, vmem_limit_bytes=56 * 1024 * 1024
        ),
        cost_estimate=pl.CostEstimate(
            flops=6 * rows * features * width, bytes_accessed=8 * depth * width, transcendentals=0
        ),
    )(tokens, norm_gain.reshape(depth_z, 1, shard), w_query, w_key, w_value, out_gain[None], carried)


def solution(mesh):
    square = mesh.shape["seq"] == 8 and mesh.shape["tensor"] == 4

    def local(tokens, *rest):
        if square and tokens.shape[0] == BLOCK:
            return fused(mesh.shape["tensor"], tokens, *rest)
        return shards(tokens, *rest)

    return jax.shard_map(
        local,
        mesh=mesh,
        in_specs=(
            P("seq", "tensor"),
            P(),
            P("seq", "tensor"),
            P("seq", "tensor"),
            P("seq", "tensor"),
            P("tensor"),
            P("tensor", None, None),
        ),
        out_specs=(P("seq", "tensor"), P("tensor", None, None)),
        check_vma=False,
    )
```
